512 devices in a mesh: lon: 128 (over x, z, y_lo), lat: 4 (over y_hi, core).
Axes of the slice: x: 4, y: 4 (y_hi: 2, y_lo: 2; y = y_hi * 2 + y_lo), z: 16, core: 2. Of those that a mesh axis runs over, the one named last changes fastest.
Arguments:
- features: bfloat16 [512, 1024, 256], P('lat', 'lon'), may hold values from -2048 to 2048
- cotangent: bfloat16 [512, 1024, 256], P('lat', 'lon'), may hold values from -96 to 96
- kernel: bfloat16 [3, 3, 256, 256], replicated, may hold values from -0.125 to 0.125
- norm_gain: float32 [256], replicated, may hold values from 0.25 to 1.75
- norm_shift: float32 [256], replicated, may hold values from -3 to 3
Outputs:
- feature_grad: bfloat16 [512, 1024, 256], P('lat', 'lon')
- kernel_grad: float32 [3, 3, 256, 256], replicated
- gain_grad: float32 [256], replicated
- shift_grad: float32 [256], replicated
The draws below stay inside these ranges and needn't reach their ends.
All inputs are finite; a program needn't handle non-finite values.
Results may differ from the reference program's by a relative error of at most 0.0024.
Values may be sent and summed in bfloat16 or wider, within the bound.
A program may use at most 64 MiB of HBM per device.

```python
import math
import jax
import jax.numpy as jnp
from jax import lax

C = 256
GROUPS = 32
LON_DEV = 8
NLAT = 512
NLON = 1024


def lon_ramp(key, count):
    position = jnp.arange(count, dtype=jnp.float32) / count
    jitter = jax.random.uniform(key, (count,), jnp.float32, -0.2, 0.2)
    return 0.316 * jnp.exp(math.log(10.0) * position + jitter)


def shared_noise(key):
    key = jax.random.fold_in(key, 101)
    return jnp.clip(jax.random.normal(key, (NLAT, NLON, C), jnp.float32), -4.0, 4.0)


def column_boost(height):
    column = jnp.arange(NLON)
    inside = (column >= NLON // 2) & (column < NLON // 2 + LON_DEV)
    channel = jnp.arange(C)
    chosen = channel < C // 4
    lifted = inside[:, None] & chosen[None, :]
    return jnp.where(lifted, height, 1.0).astype(jnp.float32)


def draw_features(key, part):
    common = shared_noise(key)
    key = jax.random.fold_in(key, 7)
    keys = jax.random.split(key, 5)
    noise = common
    along = lon_ramp(keys[1], NLON)
    offset_scale = 0.5
    across = jnp.exp(jax.random.uniform(keys[2], (C,), jnp.float32, 0.0, math.log(10.0))) / math.sqrt(10.0)
    by_row = jnp.exp(jax.random.uniform(keys[3], (NLAT, 1, 1), jnp.float32, -0.35, 0.35))
    offset = jnp.clip(jax.random.normal(keys[4], (C,), jnp.float32), -3.0, 3.0) * offset_scale
    boost = column_boost(32.0)
    value = offset * across + noise * along[None, :, None] * across * by_row * boost[None]
    return jnp.clip(value, -2048.0, 2048.0).astype(jnp.bfloat16)


def draw_cotangent(key, part):
    common = shared_noise(key)
    key = jax.random.fold_in(key, 13)
    keys = jax.random.split(key, 7)
    noise = jnp.clip(jax.random.normal(keys[0], (NLAT, NLON, C), jnp.float32), -4.0, 4.0)
    along = lon_ramp(keys[1], NLON)
    offset_scale = 0.25
    across = jnp.exp(jax.random.uniform(keys[2], (C,), jnp.float32, 0.0, math.log(10.0))) / math.sqrt(10.0)
    offset = jnp.clip(jax.random.normal(keys[3], (C,), jnp.float32), -3.0, 3.0) * offset_scale
    value = offset + noise * along[None, :, None] * across
    signs = jnp.where(jax.random.bernoulli(keys[4], 0.5, (9,)), 1.0, -1.0)
    strengths = 1.2 * signs * jax.random.uniform(keys[5], (9,), jnp.float32, 0.5, 1.0)
    order_keys = jax.random.split(keys[6], 9)
    for tap in range(9):
        tap_row = tap // 3
        tap_col = tap % 3
        order = jax.random.permutation(order_keys[tap], C)
        moved = jnp.roll(common, (1 - tap_row, 1 - tap_col), axis=(0, 1))
        value = value + strengths[tap] * jnp.take(moved, order, axis=2)
    return value.astype(jnp.bfloat16)


def normal_values(key, dims, scale, most, kind=jnp.bfloat16):
    result = jax.random.normal(key, dims, jnp.float32) * scale
    return jnp.minimum(jnp.maximum(result, -most), most).astype(kind)


def setup_inputs(seed: int = 0) -> dict:
    streams_of = jax.random.split(jax.random.key(seed), 6)
    features = draw_features(jax.random.fold_in(streams_of[5], 71), 0)
    cotangent = draw_cotangent(jax.random.fold_in(streams_of[5], 71), 0)
    kernel = normal_values(streams_of[2], (3, 3, C, C), (9 * C) ** -0.5, 0.125)
    norm_gain = jnp.clip(1.0 + 0.15 * jax.random.normal(streams_of[3], (C,), jnp.float32), 0.25, 1.75)
    norm_shift = normal_values(streams_of[4], (C,), 1.0, 3.0, jnp.float32)
    return {"features": features, "cotangent": cotangent, "kernel": kernel, "norm_gain": norm_gain, "norm_shift": norm_shift}


norm_eps = 1e-06

def group_total(per_channel, groups):
    return lax.optimization_barrier(jnp.sum(per_channel.reshape(groups, -1), axis=1))

def pole_extend(field):
    half_turn = field.shape[1] // 2
    top_row = jnp.roll(field[:1], -half_turn, axis=1)
    bottom_row = jnp.roll(field[-1:], -half_turn, axis=1)
    extended = jnp.concatenate([top_row, field, bottom_row], axis=0)
    return jnp.concatenate([extended[:, -1:], extended, extended[:, :1]], axis=1)

def pole_term(pole_row, kernel, tap_row, lon_cols, channels):
    half_turn = lon_cols // 2
    turned = jnp.roll(pole_row, -half_turn, axis=0)
    wrapped = jnp.concatenate([turned[-1:], turned, turned[:1]], axis=0)
    summed = jnp.zeros((lon_cols, channels), jnp.float32)
    for tap_col in range(3):
        window = wrapped[2 - tap_col:2 - tap_col + lon_cols]
        summed = summed + jnp.dot(window, kernel[tap_row, tap_col].T, preferred_element_type=jnp.float32)
    return summed

def reference(features, cotangent, kernel, norm_gain, norm_shift):
    lat_rows, lon_cols, channels = features.shape
    group_size = channels // GROUPS
    cell_count = lat_rows * lon_cols
    group_cells = float(cell_count * group_size)
    values = features.astype(jnp.float32)
    group_mean = group_total(lax.optimization_barrier(jnp.sum(values, axis=(0, 1))), GROUPS) / group_cells
    mean_full = jnp.repeat(group_mean, group_size)
    centered = values - mean_full
    group_var = group_total(lax.optimization_barrier(jnp.sum(centered * centered, axis=(0, 1))), GROUPS) / group_cells
    inverse_std = jnp.repeat(1.0 / jnp.sqrt(group_var + norm_eps), group_size)
    standard = centered * inverse_std
    normed = standard * norm_gain + norm_shift
    hidden = jax.nn.silu(normed).astype(jnp.bfloat16)
    padded = pole_extend(hidden)
    flat_cot = cotangent.reshape(-1, channels)
    tap_grads = []
    for tap_row in range(3):
        for tap_col in range(3):
            window = padded[tap_row:tap_row + lat_rows, tap_col:tap_col + lon_cols].reshape(-1, channels)
            tap_grads.append(jnp.dot(window.T, flat_cot, preferred_element_type=jnp.float32))
    kernel_grad = jnp.stack(tap_grads).reshape(3, 3, channels, channels) / float(cell_count)
    spread_cot = jnp.pad(cotangent, ((1, 1), (0, 0), (0, 0)))
    spread_cot = jnp.concatenate([spread_cot[:, -1:], spread_cot, spread_cot[:, :1]], axis=1)
    hidden_grad = jnp.zeros((cell_count, channels), jnp.float32)
    for tap_row in range(3):
        for tap_col in range(3):
            window = spread_cot[2 - tap_row:2 - tap_row + lat_rows, 2 - tap_col:2 - tap_col + lon_cols]
            hidden_grad = hidden_grad + jnp.dot(window.reshape(-1, channels), kernel[tap_row, tap_col].T, preferred_element_type=jnp.float32)
    hidden_grad = hidden_grad.reshape(lat_rows, lon_cols, channels)
    hidden_grad = hidden_grad.at[0].add(pole_term(cotangent[0], kernel, 0, lon_cols, channels))
    hidden_grad = hidden_grad.at[lat_rows - 1].add(pole_term(cotangent[lat_rows - 1], kernel, 2, lon_cols, channels))
    logistic = jax.nn.sigmoid(normed)
    normed_grad = hidden_grad * logistic * (1.0 + normed * (1.0 - logistic))
    gain_grad = lax.optimization_barrier(jnp.sum(normed_grad * standard, axis=(0, 1))) / float(cell_count)
    shift_grad = lax.optimization_barrier(jnp.sum(normed_grad, axis=(0, 1))) / float(cell_count)
    first_mean = jnp.repeat(group_total(norm_gain * shift_grad, GROUPS) / group_size, group_size)
    second_mean = jnp.repeat(group_total(norm_gain * gain_grad, GROUPS) / group_size, group_size)
    feature_grad = (inverse_std * (normed_grad * norm_gain - first_mean - standard * second_mean)).astype(jnp.bfloat16)
    return (feature_grad, kernel_grad, gain_grad, shift_grad)
```

```python
import jax
import jax.numpy as jnp
from jax import lax
from jax.experimental import pallas as pl
from jax.experimental.pallas import tpu as pltpu
from jax.sharding import PartitionSpec as P

MESH = pl.DeviceIdType.MESH
F32 = jnp.float32
BF16 = jnp.bfloat16

GROUP = 8
EPS = 1e-06
CH = 256
ROWS, COLS = 128, 8
CELLS = ROWS * COLS
ALL_CELLS = 512 * 1024
PARTS = 3
RED = 32
PIECE = 9 * CH // PARTS // RED
BLOCKS = 8
BLOCK = CELLS // BLOCKS


def ring(d, n):
    return min(d, n - d)


PLANE = sorted(
    [(dx, dy, dc) for dx in range(4) for dy in range(4) for dc in range(2)][1:],
    key=lambda d: -(ring(d[0], 4) + ring(d[1], 4) + 0.1 * d[2]),
)
COLUMN = sorted(range(1, 16), key=lambda d: -ring(d, 16))
SLAB = sorted(
    [(dx, dy, dz) for dx in range(4) for dy in range(4) for dz in range(2)][1:],
    key=lambda d: -(ring(d[0], 4) + ring(d[1], 4) + d[2]),
)
EVERY_OTHER = sorted(range(1, 8), key=lambda d: -ring(d, 8))


def device(x, y, z, c):
    return ((x * 16 + z) * 2 + lax.rem(y, 2), lax.div(y, 2) * 2 + c)


def wrapped(a, d, n):
    return lax.rem(a + d, n)


def over_group(v):
    lane = lax.broadcasted_iota(jnp.int32, v.shape, 1)
    for s in (1, 2, 4):
        up = pltpu.roll(v, 128 - s, 1)
        down = pltpu.roll(v, s, 1)
        v = v + jnp.where(lax.rem(lax.div(lane, s), 2) == 0, up, down)
    return v


def row(v):
    return jnp.concatenate([v[0:1], v[1:2]], axis=1)


def main_kernel(
    feat_hbm, cot_hbm, w_hbm, gain_hbm, shift_hbm,
    fg_hbm, kg_hbm, sums_hbm,
    xv, cv, wv, gv, sv, fgv,
    stage, even, odd, pole, hg, st, ds, ht,
    edge_out, edge_in, rows_out, rows_in, turn_in,
    pay1, in1, pay2, in2, spay1, sin1, spay2, sin2, sumsv,
    own, core_out, core_in, cut, cut_in, mid, mid_in, whole, whole_other,
    load_sem, out_sem, edge_s, edge_r, rows_s, rows_r,
    st_s, st_r, core_s, core_r, cut_s, cut_r, mid_s, mid_r, who_s, who_r, oth_s, oth_r,
):
    lon = lax.axis_index("lon")
    lat = lax.axis_index("lat")
    x = lax.div(lon, 32)
    z = lax.rem(lax.div(lon, 2), 16)
    y = lax.div(lat, 2) * 2 + lax.rem(lon, 2)
    c = lax.rem(lat, 2)
    zh = lax.div(z, 2)
    zl = lax.rem(z, 2)
    plane_rank = (x * 4 + y) * 2 + c
    slab_rank = (x * 4 + y) * 2 + zl
    at_top = lat == 0
    at_bottom = lat == 3
    east = (wrapped(lon, 1, 128), lat)
    west = (wrapped(lon, 127, 128), lat)
    south = (lon, wrapped(lat, 1, 4))
    north = (lon, wrapped(lat, 3, 4))
    half_turn = (wrapped(lon, 64, 128), lat)
    other_core = (lon, lat + 1 - 2 * c)

    def plane_peers():
        for dx, dy, dc in PLANE:
            yield device(wrapped(x, dx, 4), wrapped(y, dy, 4), z, lax.rem(c + dc, 2))

    def column_peers():
        for dz in COLUMN:
            yield device(x, y, wrapped(z, dz, 16), c)

    def send(src, dst, s, r, to):
        pltpu.make_async_remote_copy(
            src_ref=src, dst_ref=dst, send_sem=s, recv_sem=r,
            device_id=to, device_id_type=MESH,
        ).start()

    def take(ref, sem):
        pltpu.make_async_copy(ref, ref, sem).wait()

    def get(b, start, size):
        at = pl.ds(start, size)
        return jnp.concatenate([stage[b, 0, at, :], stage[b, 1, at, :]], axis=1)

    def put(b, start, v):
        at = pl.ds(start, v.shape[0])
        stage[b, 0, at, :] = v[:, :128]
        stage[b, 1, at, :] = v[:, 128:]

    loads = [
        pltpu.make_async_copy(src, dst, load_sem.at[i])
        for i, (src, dst) in enumerate(
            ((feat_hbm, xv), (cot_hbm, cv), (w_hbm, wv), (gain_hbm, gv), (shift_hbm, sv))
        )
    ]
    for load in loads:
        load.start()

    barrier = pltpu.get_barrier_semaphore()
    greeted = list(plane_peers()) + list(column_peers())
    for dx, dy, dz in SLAB:
        if dz == 1 and (dx, dy) != (0, 0):
            greeted.append(
                device(wrapped(x, dx, 4), wrapped(y, dy, 4), z + 1 - 2 * zl, c)
            )
    greeted += [east, west]
    for peer in greeted:
        pl.semaphore_signal(barrier, inc=1, device_id=peer, device_id_type=MESH)

    loads[0].wait()

    def add_up(i, acc):
        return acc + jnp.sum(xv[pl.ds(i * 16, 16)].astype(F32), axis=0)

    zero = jnp.zeros((COLS, CH), F32)
    total = lax.fori_loop(0, 8, add_up, zero, unroll=True)
    mean = jnp.sum(total, axis=0, keepdims=True) * (1.0 / CELLS)

    def spread(i, acc):
        d = xv[pl.ds(i * 16, 16)].astype(F32) - mean.reshape(1, 1, CH)
        return acc + jnp.sum(d * d, axis=0)

    total = lax.fori_loop(0, 8, spread, zero, unroll=True)
    dev = jnp.sum(total, axis=0, keepdims=True)
    pay1[0:1] = mean[:, :128]
    pay1[1:2] = mean[:, 128:]
    pay1[2:3] = dev[:, :128]
    pay1[3:4] = dev[:, 128:]
    in1[plane_rank] = pay1[...]

    pl.semaphore_wait(barrier, len(greeted))
    for peer in plane_peers():
        send(pay1, in1.at[plane_rank], st_s.at[0], st_r.at[0], peer)

    loads[1].wait()
    for i in range(BLOCKS):
        put(1, 8 + i * BLOCK, cv[pl.ds(i * 16, 16)].astype(F32).reshape(BLOCK, CH))
    for half in range(2):
        lanes = pl.ds(half * 128, 128)
        for side, col in ((0, 7), (1, 0)):
            v = stage[1, half, pl.ds(8 + col, ROWS, stride=8), :]
            edge_out[side, :, lanes] = v.astype(BF16)
    send(edge_out.at[0], edge_in.at[0], edge_s.at[0], edge_r.at[0], east)
    send(edge_out.at[1], edge_in.at[1], edge_s.at[1], edge_r.at[1], west)

    take(in1.at[pl.ds(0, 31)], st_r.at[0])
    v = in1[...]
    total = jnp.sum(v, axis=0)
    avg = total * (1.0 / 32)
    d = v - avg[None]
    sq = jnp.sum(d * d, axis=0)
    pay2[0:2] = avg[0:2]
    pay2[2:4] = total[2:4] + float(CELLS) * sq[0:2]
    in2[z] = pay2[...]
    for peer in column_peers():
        send(pay2, in2.at[z], st_s.at[1], st_r.at[1], peer)

    for i in range(BLOCKS):
        lo = 8 + i * BLOCK
        v = get(1, lo, BLOCK)
        even[1, pl.ds(i * BLOCK, BLOCK), :] = v.astype(BF16)
        put(2, lo, pltpu.roll(v, 1, 0))
        put(0, lo, pltpu.roll(v, BLOCK - 1, 0))
    take(edge_in.at[0], edge_r.at[0])
    take(edge_in.at[1], edge_r.at[1])
    for half in range(2):
        lanes = pl.ds(half * 128, 128)
        for b, side, col in ((2, 0, 0), (0, 1, 7)):
            v = edge_in[side, :, lanes].astype(F32)
            stage[b, half, pl.ds(8 + col, ROWS, stride=8), :] = v
    for b in range(3):
        rows_out[0, b] = get(b, 8, 8)
        rows_out[1, b] = get(b, CELLS, 8)
    send(rows_out.at[0], rows_in.at[1], rows_s.at[0], rows_r.at[0], north)
    send(rows_out.at[1], rows_in.at[0], rows_s.at[1], rows_r.at[1], south)
    send(rows_out, turn_in, rows_s.at[2], rows_r.at[2], half_turn)
    for b in (0, 2):
        even[b] = get(b, 8, CELLS).astype(BF16)
    pole[...] = jnp.zeros_like(pole)
    take(rows_in.at[1], rows_r.at[0])
    take(rows_in.at[0], rows_r.at[1])
    take(turn_in, rows_r.at[2])
    for b in range(3):
        put(b, 0, jnp.where(at_top, 0.0, rows_in[0, b]))
        put(b, 8 + CELLS, jnp.where(at_bottom, 0.0, rows_in[1, b]))
        odd[b] = get(b, 0, CELLS + 16).astype(BF16)
        pole[b, pl.ds(0, 16), :] = jnp.concatenate(
            [
                jnp.where(at_top, turn_in[0, b], 0.0),
                jnp.where(at_bottom, turn_in[1, b], 0.0),
            ],
            axis=0,
        ).astype(BF16)

    def window(a, b, start, size):
        if a == 0:
            return odd[b, pl.ds(16 + start, size), :]
        if a == 1:
            return even[b, pl.ds(start, size), :]
        return odd[b, pl.ds(start, size), :]

    loads[2].wait()
    contract_last = (((1,), (1,)), ((), ()))
    for i in range(4):
        acc = None
        for a in range(3):
            for b in range(3):
                part = lax.dot_general(
                    window(a, b, i * 256, 256), wv[a * 3 + b], contract_last,
                    preferred_element_type=F32,
                )
                acc = part if acc is None else acc + part
        hg[pl.ds(i * 256, 256), :] = acc
    for a, at in ((0, 0), (2, 1)):
        acc = None
        for b in range(3):
            part = lax.dot_general(
                pole[b, pl.ds(0, 16), :], wv[a * 3 + b], contract_last,
                preferred_element_type=F32,
            )
            acc = part if acc is None else acc + part
        where = pl.ds(0, 8) if at == 0 else pl.ds(CELLS - 8, 8)
        hg[where, :] = hg[where, :] + acc[at * 8 : at * 8 + 8]

    loads[3].wait()
    loads[4].wait()
    take(in2.at[pl.ds(0, 15)], st_r.at[1])
    v = in2[...]
    total = jnp.sum(v, axis=0)
    avg = total * (1.0 / 16)
    d = v - avg[None]
    sq = jnp.sum(d * d, axis=0)
    ch_mean = avg[0:2]
    ch_dev = total[2:4] + float(CELLS * 32) * sq[0:2]
    g_mean = over_group(ch_mean) * (1.0 / GROUP)
    off = ch_mean - g_mean
    g_var = over_group(ch_dev + float(ALL_CELLS) * off * off) * (
        1.0 / (GROUP * ALL_CELLS)
    )
    inv = row(1.0 / jnp.sqrt(g_var + EPS))
    mean = row(g_mean)
    gain = gv[...].reshape(1, CH)
    shift = sv[...].reshape(1, CH)

    for i in range(BLOCKS):
        at = pl.ds(i * BLOCK, BLOCK)
        s0 = (xv[pl.ds(i * 16, 16)].astype(F32).reshape(BLOCK, CH) - mean) * inv
        nm = s0 * gain + shift
        s = 1.0 / (1.0 + jnp.exp(jnp.minimum(-nm, 87.0)))
        h = (nm * s).astype(BF16)
        st[at, :] = s0
        ds[at, :] = s * (1.0 + nm * (1.0 - s))
        ht[:, at] = h.T
        if i == 0:
            first = h[0:16]
        if i == BLOCKS - 1:
            last = h[BLOCK - 16 : BLOCK]
    keep = lax.broadcasted_iota(jnp.int32, (128, CH), 0)
    zeros = jnp.zeros((112, CH), BF16)
    first = jnp.concatenate([first, zeros], axis=0).astype(F32)
    last = jnp.concatenate([last, zeros], axis=0).astype(F32)
    first_t = jnp.where(keep < 8, first, 0.0).astype(BF16).T
    last_t = jnp.where((keep >= 8) & (keep < 16), last, 0.0).astype(BF16).T

    def partial(p):
        for b in range(3):
            r = jnp.dot(ht[...], window(p, b, 0, CELLS), preferred_element_type=F32)
            if p == 0:
                r = r + jnp.dot(first_t, pole[b], preferred_element_type=F32)
            if p == 2:
                r = r + jnp.dot(last_t, pole[b], preferred_element_type=F32)
            at = pl.ds(b * CH, CH)
            own[p, at, :] = jnp.where(c == 0, r[:, :128], r[:, 128:])
            core_out[p, at, :] = jnp.where(c == 0, r[:, 128:], r[:, :128]).astype(BF16)
        send(core_out.at[p], core_in.at[p], core_s.at[p], core_r.at[p], other_core)

    def scatter(p):
        take(core_in.at[p], core_r.at[p])
        v = own[p] + core_in[p].astype(F32)
        cut[p] = v.reshape(RED, PIECE, 128).astype(BF16)
        cut_in[p, slab_rank] = cut[p, slab_rank]
        for dx, dy, dz in SLAB:
            px, py = wrapped(x, dx, 4), wrapped(y, dy, 4)
            pz = lax.rem(zl + dz, 2)
            rank = (px * 4 + py) * 2 + pz
            send(
                cut.at[p, rank], cut_in.at[p, slab_rank], cut_s.at[p], cut_r.at[p],
                device(px, py, zh * 2 + pz, c),
            )

    def exchange(p):
        take(cut_in.at[p, pl.ds(0, RED - 1)], cut_r.at[p])
        v = jnp.sum(cut_in[p].astype(F32), axis=0).astype(BF16)
        mid[p] = v
        mid_in[p, zh] = v
        for d in EVERY_OTHER:
            send(
                mid.at[p], mid_in.at[p, zh], mid_s.at[p], mid_r.at[p],
                device(x, y, wrapped(zh, d, 8) * 2 + zl, c),
            )

    def gather(p):
        take(mid_in.at[p, pl.ds(0, 7)], mid_r.at[p])
        v = jnp.sum(mid_in[p].astype(F32), axis=0) * (1.0 / ALL_CELLS)
        whole[p, slab_rank] = v.astype(BF16)
        for dx, dy, dz in SLAB:
            px, py = wrapped(x, dx, 4), wrapped(y, dy, 4)
            send(
                whole.at[p, slab_rank], whole.at[p, slab_rank], who_s.at[p], who_r.at[p],
                device(px, py, zh * 2 + lax.rem(zl + dz, 2), c),
            )

    def hand_over(p):
        take(whole.at[p, pl.ds(0, RED - 1)], who_r.at[p])
        send(whole.at[p], whole_other.at[p], oth_s.at[p], oth_r.at[p], other_core)
        pltpu.make_async_copy(whole.at[p], kg_hbm.at[p, c], out_sem.at[p]).start()

    partial(0)
    partial(1)
    scatter(0)
    partial(2)
    scatter(1)
    scatter(2)

    acc1 = zero
    acc2 = zero
    for i in range(BLOCKS):
        at = pl.ds(i * BLOCK, BLOCK)
        ng = hg[at, :] * ds[at, :]
        hg[at, :] = ng
        acc1 = acc1 + jnp.sum(ng.reshape(16, 8, CH), axis=0)
        acc2 = acc2 + jnp.sum((ng * st[at, :]).reshape(16, 8, CH), axis=0)
    s1 = jnp.sum(acc1, axis=0, keepdims=True)
    s2 = jnp.sum(acc2, axis=0, keepdims=True)
    spay1[0:1] = s1[:, :128]
    spay1[1:2] = s1[:, 128:]
    spay1[2:3] = s2[:, :128]
    spay1[3:4] = s2[:, 128:]
    sin1[plane_rank] = spay1[...]
    for peer in plane_peers():
        send(spay1, sin1.at[plane_rank], st_s.at[2], st_r.at[2], peer)

    exchange(0)
    exchange(1)
    take(sin1.at[pl.ds(0, 31)], st_r.at[2])
    spay2[...] = jnp.sum(sin1[...], axis=0)
    sin2[z] = spay2[...]
    for peer in column_peers():
        send(spay2, sin2.at[z], st_s.at[3], st_r.at[3], peer)
    exchange(2)
    for p in range(PARTS):
        gather(p)

    take(sin2.at[pl.ds(0, 15)], st_r.at[3])
    grads = jnp.sum(sin2[...], axis=0) * (1.0 / ALL_CELLS)
    sumsv[...] = grads
    to_sums = pltpu.make_async_copy(sumsv, sums_hbm, out_sem.at[PARTS])
    to_sums.start()
    gain2 = jnp.concatenate([gain[:, :128], gain[:, 128:]], axis=0)
    m1 = row(over_group(gain2 * grads[0:2]) * (1.0 / GROUP))
    m2 = row(over_group(gain2 * grads[2:4]) * (1.0 / GROUP))
    for i in range(BLOCKS):
        at = pl.ds(i * BLOCK, BLOCK)
        v = inv * (hg[at, :] * gain - m1 - st[at, :] * m2)
        fgv[pl.ds(i * 16, 16)] = v.reshape(16, 8, CH).astype(BF16)
    to_fg = pltpu.make_async_copy(fgv, fg_hbm, out_sem.at[PARTS + 1])
    to_fg.start()

    for p in range(PARTS):
        hand_over(p)
    outs = []
    for p in range(PARTS):
        take(whole_other.at[p], oth_r.at[p])
        out = pltpu.make_async_copy(
            whole_other.at[p], kg_hbm.at[p, 1 - c], out_sem.at[PARTS + 2 + p]
        )
        out.start()
        outs.append(out)

    take(edge_out.at[0], edge_s.at[0])
    take(edge_out.at[1], edge_s.at[1])
    take(rows_out.at[0], rows_s.at[0])
    take(rows_out.at[1], rows_s.at[1])
    take(rows_out, rows_s.at[2])
    take(in1.at[pl.ds(0, 31)], st_s.at[0])
    take(in2.at[pl.ds(0, 15)], st_s.at[1])
    take(sin1.at[pl.ds(0, 31)], st_s.at[2])
    take(sin2.at[pl.ds(0, 15)], st_s.at[3])
    for p in range(PARTS):
        take(core_out.at[p], core_s.at[p])
        take(cut.at[p, pl.ds(0, RED - 1)], cut_s.at[p])
        take(mid_in.at[p, pl.ds(0, 7)], mid_s.at[p])
        take(whole.at[p, pl.ds(0, RED - 1)], who_s.at[p])
        take(whole.at[p], oth_s.at[p])
        pltpu.make_async_copy(whole.at[p], kg_hbm.at[p, c], out_sem.at[p]).wait()
    to_sums.wait()
    to_fg.wait()
    for out in outs:
        out.wait()


def last_kernel(kg, fg_hbm, sums, kgrad, fg_out, gain_grad, shift_grad, sem):
    copy = pltpu.make_async_copy(fg_hbm, fg_out, sem)

    @pl.when(pl.program_id(0) == 0)
    def _():
        copy.start()
        for half in range(2):
            at = pl.ds(half * 128, 128)
            shift_grad[at] = sums[half]
            gain_grad[at] = sums[2 + half]

    for half in range(2):
        v = kg[0, half].astype(F32).reshape(RED * PIECE, 128)
        kgrad[:, pl.ds(half * 128, 128)] = v

    @pl.when(pl.program_id(0) == PARTS - 1)
    def _():
        copy.wait()


def local(features, cotangent, kernel, norm_gain, norm_shift):
    any_spec = pl.BlockSpec(memory_space=pl.ANY)
    vmem = pltpu.VMEM
    dma = pltpu.SemaphoreType.DMA
    features, cotangent, kernel, norm_gain, norm_shift = [
        pltpu.with_memory_space_constraint(v, pltpu.HBM)
        for v in (features, cotangent, kernel.reshape(9, CH, CH), norm_gain, norm_shift)
    ]
    fg, kg, sums = pl.pallas_call(
        main_kernel,
        out_shape=(
            jax.ShapeDtypeStruct((ROWS, COLS, CH), BF16),
            jax.ShapeDtypeStruct((PARTS, 2, RED, PIECE, 128), BF16),
            jax.ShapeDtypeStruct((4, 128), F32),
        ),
        in_specs=[pl.BlockSpec(memory_space=pltpu.HBM)] * 5,
        out_specs=(any_spec,) * 3,
        scratch_shapes=[
            vmem((ROWS, COLS, CH), BF16),
            vmem((ROWS, COLS, CH), BF16),
            vmem((9, CH, CH), BF16),
            vmem((CH,), F32),
            vmem((CH,), F32),
            vmem((ROWS, COLS, CH), BF16),
            vmem((3, 2, CELLS + 16, 128), F32),
            vmem((3, CELLS, CH), BF16),
            vmem((3, CELLS + 16, CH), BF16),
            vmem((3, 128, CH), BF16),
            vmem((CELLS, CH), F32),
            vmem((CELLS, CH), F32),
            vmem((CELLS, CH), F32),
            vmem((CH, CELLS), BF16),
            vmem((2, ROWS, CH), BF16),
            vmem((2, ROWS, CH), BF16),
            vmem((2, 3, 8, CH), F32),
            vmem((2, 3, 8, CH), F32),
            vmem((2, 3, 8, CH), F32),
            vmem((4, 128), F32),
            vmem((32, 4, 128), F32),
            vmem((4, 128), F32),
            vmem((16, 4, 128), F32),
            vmem((4, 128), F32),
            vmem((32, 4, 128), F32),
            vmem((4, 128), F32),
            vmem((16, 4, 128), F32),
            vmem((4, 128), F32),
            vmem((PARTS, RED * PIECE, 128), F32),
            vmem((PARTS, RED * PIECE, 128), BF16),
            vmem((PARTS, RED * PIECE, 128), BF16),
            vmem((PARTS, RED, PIECE, 128), BF16),
            vmem((PARTS, RED, PIECE, 128), BF16),
            vmem((PARTS, PIECE, 128), BF16),
            vmem((PARTS, 8, PIECE, 128), BF16),
            vmem((PARTS, RED, PIECE, 128), BF16),
            vmem((PARTS, RED, PIECE, 128), BF16),
            dma((5,)),
            dma((2 * PARTS + 2,)),
            dma((2,)), dma((2,)),
            dma((3,)), dma((3,)),
            dma((4,)), dma((4,)),
            dma((PARTS,)), dma((PARTS,)),
            dma((PARTS,)), dma((PARTS,)),
            dma((PARTS,)), dma((PARTS,)),
            dma((PARTS,)), dma((PARTS,)),
            dma((PARTS,)), dma((PARTS,)),
        ],
        compiler_params=pltpu.CompilerParams(
            collective_id=0, has_side_effects=True, vmem_limit_bytes=48 * 2**20
        ),
        name="backward",
    )(features, cotangent, kernel, norm_gain, norm_shift)
    kgrad, fg, gain_grad, shift_grad = pl.pallas_call(
        last_kernel,
        grid=(PARTS,),
        out_shape=(
            jax.ShapeDtypeStruct((9 * CH, CH), F32),
            jax.ShapeDtypeStruct((ROWS, COLS, CH), BF16),
            jax.ShapeDtypeStruct((CH,), F32),
            jax.ShapeDtypeStruct((CH,), F32),
        ),
        in_specs=[
            pl.BlockSpec((1, 2, RED, PIECE, 128), lambda i: (i, 0, 0, 0, 0)),
            any_spec,
            pl.BlockSpec((4, 128), lambda i: (0, 0)),
        ],
        out_specs=(
            pl.BlockSpec((RED * PIECE, CH), lambda i: (i, 0)),
            any_spec,
            pl.BlockSpec((CH,), lambda i: (0,)),
            pl.BlockSpec((CH,), lambda i: (0,)),
        ),
        scratch_shapes=[dma],
        compiler_params=pltpu.CompilerParams(vmem_limit_bytes=16 * 2**20),
        name="outputs",
    )(kg, fg, sums)
    return fg, kgrad.reshape(3, 3, CH, CH), gain_grad, shift_grad


def solution(mesh):
    placed = (P("lat", "lon", None), P("lat", "lon", None), P(), P(), P())
    return jax.shard_map(
        local,
        mesh=mesh,
        in_specs=placed,
        out_specs=(P("lat", "lon", None), P(), P(), P()),
        check_vma=False,
    )
```

```python
import jax
import jax.numpy as jnp
from jax import lax
from jax.experimental import pallas as pl
from jax.experimental.pallas import tpu as pltpu
from jax.sharding import PartitionSpec as P

MESH = pl.DeviceIdType.MESH
F32 = jnp.float32
BF16 = jnp.bfloat16

GROUP = 8
EPS = 1e-06
CH = 256
ROWS, COLS = 128, 8
CELLS = ROWS * COLS
ALL_CELLS = 512 * 1024
PARTS = 3
RED = 32
PIECE = 9 * CH // PARTS // RED
BLOCKS = 8
BLOCK = CELLS // BLOCKS


def ring(d, n):
    return min(d, n - d)


PLANE = sorted(
    [(dx, dy, dc) for dx in range(4) for dy in range(4) for dc in range(2)][1:],
    key=lambda d: -(ring(d[0], 4) + ring(d[1], 4) + 0.1 * d[2]),
)
COLUMN = sorted(range(1, 16), key=lambda d: -ring(d, 16))
SLAB = sorted(
    [(dx, dy, dz) for dx in range(4) for dy in range(4) for dz in range(2)][1:],
    key=lambda d: -(ring(d[0], 4) + ring(d[1], 4) + d[2]),
)
EVERY_OTHER = sorted(range(1, 8), key=lambda d: -ring(d, 8))


def device(x, y, z, c):
    return ((x * 16 + z) * 2 + lax.rem(y, 2), lax.div(y, 2) * 2 + c)


def wrapped(a, d, n):
    return lax.rem(a + d, n)


def over_group(v):
    lane = lax.broadcasted_iota(jnp.int32, v.shape, 1)
    for s in (1, 2, 4):
        up = pltpu.roll(v, 128 - s, 1)
        down = pltpu.roll(v, s, 1)
        v = v + jnp.where(lax.rem(lax.div(lane, s), 2) == 0, up, down)
    return v


def row(v):
    return jnp.concatenate([v[0:1], v[1:2]], axis=1)


def main_kernel(
    feat_hbm, cot_hbm, w_hbm, gain_hbm, shift_hbm,
    fg_hbm, kg_hbm, sums_hbm,
    xv, cv, wv, gv, sv, fgv,
    stage, even, odd, pole, hg, ht,
    edge_out, edge_in, rows_out, rows_in, turn_in,
    pay1, in1, pay2, in2, spay1, sin1, spay2, sin2, sumsv,
    own, core_out, core_in, cut, cut_in, mid, mid_in, whole, whole_other,
    relay_sem, load_sem, out_sem, edge_s, edge_r, rows_s, rows_r,
    st_s, st_r, core_s, core_r, cut_s, cut_r, mid_s, mid_r, who_s, who_r, oth_s, oth_r,
):
    lon = lax.axis_index("lon")
    lat = lax.axis_index("lat")
    x = lax.div(lon, 32)
    z = lax.rem(lax.div(lon, 2), 16)
    y = lax.div(lat, 2) * 2 + lax.rem(lon, 2)
    c = lax.rem(lat, 2)
    zh = lax.div(z, 2)
    zl = lax.rem(z, 2)
    plane_rank = (x * 4 + y) * 2 + c
    slab_rank = (x * 4 + y) * 2 + zl
    at_top = lat == 0
    at_bottom = lat == 3
    east = (wrapped(lon, 1, 128), lat)
    west = (wrapped(lon, 127, 128), lat)
    south = (lon, wrapped(lat, 1, 4))
    north = (lon, wrapped(lat, 3, 4))
    half_turn = (wrapped(lon, 64, 128), lat)
    other_core = (lon, lat + 1 - 2 * c)

    def plane_peers():
        for dx, dy, dc in PLANE:
            yield device(wrapped(x, dx, 4), wrapped(y, dy, 4), z, lax.rem(c + dc, 2))

    def column_peers():
        for dz in COLUMN:
            yield device(x, y, wrapped(z, dz, 16), c)

    def send(src, dst, s, r, to):
        pltpu.make_async_remote_copy(
            src_ref=src, dst_ref=dst, send_sem=s, recv_sem=r,
            device_id=to, device_id_type=MESH,
        ).start()

    def take(ref, sem):
        pltpu.make_async_copy(ref, ref, sem).wait()

    def get(b, start, size):
        at = pl.ds(start, size)
        return jnp.concatenate([stage[b, 0, at, :], stage[b, 1, at, :]], axis=1)

    def put(b, start, v):
        at = pl.ds(start, v.shape[0])
        stage[b, 0, at, :] = v[:, :128]
        stage[b, 1, at, :] = v[:, 128:]

    loads = [
        pltpu.make_async_copy(src, dst, load_sem.at[i])
        for i, (src, dst) in enumerate(
            ((feat_hbm, xv), (cot_hbm, cv), (w_hbm, wv), (gain_hbm, gv), (shift_hbm, sv))
        )
    ]
    loads[0].start()

    barrier = pltpu.get_barrier_semaphore()
    greeted = [device(x, y, wrapped(z, d, 16), c) for d in (4, 12)]
    for dx, dy, dz in SLAB:
        if dz == 1 and (dx, dy) != (0, 0):
            greeted.append(
                device(wrapped(x, dx, 4), wrapped(y, dy, 4), z + 1 - 2 * zl, c)
            )
    greeted += list(plane_peers())
    greeted += [device(x, y, wrapped(z, d, 16), c) for d in (3, 13, 2, 14, 1, 15)]
    greeted += [east, west]
    for peer in greeted:
        pl.semaphore_signal(barrier, inc=1, device_id=peer, device_id_type=MESH)
    for load in loads[1:]:
        load.start()

    loads[0].wait()

    def add_up(i, acc):
        return acc + jnp.sum(xv[pl.ds(i * 16, 16)].astype(F32), axis=0)

    zero = jnp.zeros((COLS, CH), F32)
    total = lax.fori_loop(0, 8, add_up, zero, unroll=True)
    mean = jnp.sum(total, axis=0, keepdims=True) * (1.0 / CELLS)

    def spread(i, acc):
        d = xv[pl.ds(i * 16, 16)].astype(F32) - mean.reshape(1, 1, CH)
        return acc + jnp.sum(d * d, axis=0)

    total = lax.fori_loop(0, 8, spread, zero, unroll=True)
    dev = jnp.sum(total, axis=0, keepdims=True)
    pay1[0:1] = mean[:, :128]
    pay1[1:2] = mean[:, 128:]
    pay1[2:3] = dev[:, :128]
    pay1[3:4] = dev[:, 128:]
    in1[plane_rank] = pay1[...]

    pl.semaphore_wait(barrier, len(greeted))
    for d in (4, 12):
        pl.semaphore_signal(
            relay_sem, inc=1, device_id=device(x, y, wrapped(z, d, 16), c),
            device_id_type=MESH,
        )
    for peer in plane_peers():
        send(pay1, in1.at[plane_rank], st_s.at[0], st_r.at[0], peer)

    loads[1].wait()
    for i in range(BLOCKS):
        put(1, 8 + i * BLOCK, cv[pl.ds(i * 16, 16)].astype(F32).reshape(BLOCK, CH))
    for half in range(2):
        lanes = pl.ds(half * 128, 128)
        for side, col in ((0, 7), (1, 0)):
            v = stage[1, half, pl.ds(8 + col, ROWS, stride=8), :]
            edge_out[side, :, lanes] = v.astype(BF16)
    send(edge_out.at[0], edge_in.at[0], edge_s.at[0], edge_r.at[0], east)
    send(edge_out.at[1], edge_in.at[1], edge_s.at[1], edge_r.at[1], west)

    take(in1.at[pl.ds(0, 31)], st_r.at[0])
    v = in1[...]
    total = jnp.sum(v, axis=0)
    avg = total * (1.0 / 32)
    d = v - avg[None]
    sq = jnp.sum(d * d, axis=0)
    pay2[0:2] = avg[0:2]
    pay2[2:4] = total[2:4] + float(CELLS) * sq[0:2]
    in2[z] = pay2[...]
    pl.semaphore_wait(relay_sem, 2)
    for peer in column_peers():
        send(pay2, in2.at[z], st_s.at[1], st_r.at[1], peer)

    for i in range(BLOCKS):
        lo = 8 + i * BLOCK
        v = get(1, lo, BLOCK)
        even[1, pl.ds(i * BLOCK, BLOCK), :] = v.astype(BF16)
        put(2, lo, pltpu.roll(v, 1, 0))
        put(0, lo, pltpu.roll(v, BLOCK - 1, 0))
    take(edge_in.at[0], edge_r.at[0])
    take(edge_in.at[1], edge_r.at[1])
    for half in range(2):
        lanes = pl.ds(half * 128, 128)
        for b, side, col in ((2, 0, 0), (0, 1, 7)):
            v = edge_in[side, :, lanes].astype(F32)
            stage[b, half, pl.ds(8 + col, ROWS, stride=8), :] = v
    for b in range(3):
        rows_out[0, b] = get(b, 8, 8)
        rows_out[1, b] = get(b, CELLS, 8)
    send(rows_out.at[0], rows_in.at[1], rows_s.at[0], rows_r.at[0], north)
    send(rows_out.at[1], rows_in.at[0], rows_s.at[1], rows_r.at[1], south)
    send(rows_out, turn_in, rows_s.at[2], rows_r.at[2], half_turn)
    for b in (0, 2):
        even[b] = get(b, 8, CELLS).astype(BF16)
    pole[...] = jnp.zeros_like(pole)
    take(rows_in.at[1], rows_r.at[0])
    take(rows_in.at[0], rows_r.at[1])
    take(turn_in, rows_r.at[2])
    for b in range(3):
        put(b, 0, jnp.where(at_top, 0.0, rows_in[0, b]))
        put(b, 8 + CELLS, jnp.where(at_bottom, 0.0, rows_in[1, b]))
        odd[b] = get(b, 0, CELLS + 16).astype(BF16)
        pole[b, pl.ds(0, 16), :] = jnp.concatenate(
            [
                jnp.where(at_top, turn_in[0, b], 0.0),
                jnp.where(at_bottom, turn_in[1, b], 0.0),
            ],
            axis=0,
        ).astype(BF16)

    def window(a, b, start, size):
        if a == 0:
            return odd[b, pl.ds(16 + start, size), :]
        if a == 1:
            return even[b, pl.ds(start, size), :]
        return odd[b, pl.ds(start, size), :]

    loads[2].wait()
    contract_last = (((1,), (1,)), ((), ()))
    for i in range(4):
        acc = None
        for a in range(3):
            for b in range(3):
                part = lax.dot_general(
                    window(a, b, i * 256, 256), wv[a * 3 + b], contract_last,
                    preferred_element_type=F32,
                )
                acc = part if acc is None else acc + part
        hg[pl.ds(i * 256, 256), :] = acc
    for a, at in ((0, 0), (2, 1)):
        acc = None
        for b in range(3):
            part = lax.dot_general(
                pole[b, pl.ds(0, 16), :], wv[a * 3 + b], contract_last,
                preferred_element_type=F32,
            )
            acc = part if acc is None else acc + part
        where = pl.ds(0, 8) if at == 0 else pl.ds(CELLS - 8, 8)
        hg[where, :] = hg[where, :] + acc[at * 8 : at * 8 + 8]

    loads[3].wait()
    loads[4].wait()
    take(in2.at[pl.ds(0, 15)], st_r.at[1])
    v = in2[...]
    total = jnp.sum(v, axis=0)
    avg = total * (1.0 / 16)
    d = v - avg[None]
    sq = jnp.sum(d * d, axis=0)
    ch_mean = avg[0:2]
    ch_dev = total[2:4] + float(CELLS * 32) * sq[0:2]
    g_mean = over_group(ch_mean) * (1.0 / GROUP)
    off = ch_mean - g_mean
    g_var = over_group(ch_dev + float(ALL_CELLS) * off * off) * (
        1.0 / (GROUP * ALL_CELLS)
    )
    inv = row(1.0 / jnp.sqrt(g_var + EPS))
    mean = row(g_mean)
    gain = gv[...].reshape(1, CH)
    shift = sv[...].reshape(1, CH)

    def standard(i):
        return (xv[pl.ds(i * 16, 16)].astype(F32).reshape(BLOCK, CH) - mean) * inv

    def logistic(v):
        d = 1.0 + jnp.exp(jnp.minimum(-v, 87.0))
        r = pl.reciprocal(d, approx=True)
        return r * (2.0 - d * r)

    for i in range(BLOCKS):
        at = pl.ds(i * BLOCK, BLOCK)
        nm = standard(i) * gain + shift
        h = (nm * logistic(nm)).astype(BF16)
        ht[:, at] = h.T
        if i == 0:
            first = h[0:16]
        if i == BLOCKS - 1:
            last = h[BLOCK - 16 : BLOCK]
    keep = lax.broadcasted_iota(jnp.int32, (128, CH), 0)
    zeros = jnp.zeros((112, CH), BF16)
    first = jnp.concatenate([first, zeros], axis=0).astype(F32)
    last = jnp.concatenate([last, zeros], axis=0).astype(F32)
    first_t = jnp.where(keep < 8, first, 0.0).astype(BF16).T
    last_t = jnp.where((keep >= 8) & (keep < 16), last, 0.0).astype(BF16).T

    def partial(p):
        for b in range(3):
            r = jnp.dot(ht[...], window(p, b, 0, CELLS), preferred_element_type=F32)
            if p == 0:
                r = r + jnp.dot(first_t, pole[b], preferred_element_type=F32)
            if p == 2:
                r = r + jnp.dot(last_t, pole[b], preferred_element_type=F32)
            at = pl.ds(b * CH, CH)
            own[p, at, :] = jnp.where(c == 0, r[:, :128], r[:, 128:])
            core_out[p, at, :] = jnp.where(c == 0, r[:, 128:], r[:, :128]).astype(BF16)
        send(core_out.at[p], core_in.at[p], core_s.at[p], core_r.at[p], other_core)

    def scatter(p):
        take(core_in.at[p], core_r.at[p])
        v = own[p] + core_in[p].astype(F32)
        cut[p] = v.reshape(RED, PIECE, 128).astype(BF16)
        cut_in[p, slab_rank] = cut[p, slab_rank]
        for dx, dy, dz in SLAB:
            px, py = wrapped(x, dx, 4), wrapped(y, dy, 4)
            pz = lax.rem(zl + dz, 2)
            rank = (px * 4 + py) * 2 + pz
            send(
                cut.at[p, rank], cut_in.at[p, slab_rank], cut_s.at[p], cut_r.at[p],
                device(px, py, zh * 2 + pz, c),
            )

    def exchange(p):
        take(cut_in.at[p, pl.ds(0, RED - 1)], cut_r.at[p])
        v = jnp.sum(cut_in[p].astype(F32), axis=0).astype(BF16)
        mid[p] = v
        mid_in[p, zh] = v
        for d in EVERY_OTHER:
            send(
                mid.at[p], mid_in.at[p, zh], mid_s.at[p], mid_r.at[p],
                device(x, y, wrapped(zh, d, 8) * 2 + zl, c),
            )

    def gather(p):
        take(mid_in.at[p, pl.ds(0, 7)], mid_r.at[p])
        v = jnp.sum(mid_in[p].astype(F32), axis=0) * (1.0 / ALL_CELLS)
        whole[p, slab_rank] = v.astype(BF16)
        for dx, dy, dz in SLAB:
            px, py = wrapped(x, dx, 4), wrapped(y, dy, 4)
            send(
                whole.at[p, slab_rank], whole.at[p, slab_rank], who_s.at[p], who_r.at[p],
                device(px, py, zh * 2 + lax.rem(zl + dz, 2), c),
            )

    def hand_over(p):
        take(whole.at[p, pl.ds(0, RED - 1)], who_r.at[p])
        send(whole.at[p], whole_other.at[p], oth_s.at[p], oth_r.at[p], other_core)
        pltpu.make_async_copy(whole.at[p], kg_hbm.at[p, c], out_sem.at[p]).start()

    partial(0)
    partial(1)
    scatter(0)
    partial(2)
    scatter(1)
    scatter(2)

    acc1 = zero
    acc2 = zero
    for i in range(BLOCKS):
        at = pl.ds(i * BLOCK, BLOCK)
        s0 = standard(i)
        nm = s0 * gain + shift
        s = logistic(nm)
        ng = hg[at, :] * (s * (1.0 + nm * (1.0 - s)))
        hg[at, :] = ng
        acc1 = acc1 + jnp.sum(ng.reshape(16, 8, CH), axis=0)
        acc2 = acc2 + jnp.sum((ng * s0).reshape(16, 8, CH), axis=0)
    s1 = jnp.sum(acc1, axis=0, keepdims=True)
    s2 = jnp.sum(acc2, axis=0, keepdims=True)
    spay1[0:1] = s1[:, :128]
    spay1[1:2] = s1[:, 128:]
    spay1[2:3] = s2[:, :128]
    spay1[3:4] = s2[:, 128:]
    sin1[plane_rank] = spay1[...]
    for peer in plane_peers():
        send(spay1, sin1.at[plane_rank], st_s.at[2], st_r.at[2], peer)

    exchange(0)
    exchange(1)
    exchange(2)
    take(sin1.at[pl.ds(0, 31)], st_r.at[2])
    spay2[...] = jnp.sum(sin1[...], axis=0)
    sin2[z] = spay2[...]
    for peer in column_peers():
        send(spay2, sin2.at[z], st_s.at[3], st_r.at[3], peer)
    for p in range(PARTS):
        gather(p)

    take(sin2.at[pl.ds(0, 15)], st_r.at[3])
    grads = jnp.sum(sin2[...], axis=0) * (1.0 / ALL_CELLS)
    sumsv[...] = grads
    to_sums = pltpu.make_async_copy(sumsv, sums_hbm, out_sem.at[PARTS])
    to_sums.start()
    gain2 = jnp.concatenate([gain[:, :128], gain[:, 128:]], axis=0)
    m1 = row(over_group(gain2 * grads[0:2]) * (1.0 / GROUP))
    m2 = row(over_group(gain2 * grads[2:4]) * (1.0 / GROUP))
    for i in range(BLOCKS):
        at = pl.ds(i * BLOCK, BLOCK)
        v = inv * (hg[at, :] * gain - m1 - standard(i) * m2)
        fgv[pl.ds(i * 16, 16)] = v.reshape(16, 8, CH).astype(BF16)
    to_fg = pltpu.make_async_copy(fgv, fg_hbm, out_sem.at[PARTS + 1])
    to_fg.start()

    for p in range(PARTS):
        hand_over(p)
    outs = []
    for p in range(PARTS):
        take(whole_other.at[p], oth_r.at[p])
        out = pltpu.make_async_copy(
            whole_other.at[p], kg_hbm.at[p, 1 - c], out_sem.at[PARTS + 2 + p]
        )
        out.start()
        outs.append(out)

    take(edge_out.at[0], edge_s.at[0])
    take(edge_out.at[1], edge_s.at[1])
    take(rows_out.at[0], rows_s.at[0])
    take(rows_out.at[1], rows_s.at[1])
    take(rows_out, rows_s.at[2])
    take(in1.at[pl.ds(0, 31)], st_s.at[0])
    take(in2.at[pl.ds(0, 15)], st_s.at[1])
    take(sin1.at[pl.ds(0, 31)], st_s.at[2])
    take(sin2.at[pl.ds(0, 15)], st_s.at[3])
    for p in range(PARTS):
        take(core_out.at[p], core_s.at[p])
        take(cut.at[p, pl.ds(0, RED - 1)], cut_s.at[p])
        take(mid_in.at[p, pl.ds(0, 7)], mid_s.at[p])
        take(whole.at[p, pl.ds(0, RED - 1)], who_s.at[p])
        take(whole.at[p], oth_s.at[p])
        pltpu.make_async_copy(whole.at[p], kg_hbm.at[p, c], out_sem.at[p]).wait()
    to_sums.wait()
    to_fg.wait()
    for out in outs:
        out.wait()


def last_kernel(kg, fg_hbm, sums, kgrad, fg_out, gain_grad, shift_grad, sem):
    copy = pltpu.make_async_copy(fg_hbm, fg_out, sem)

    @pl.when(pl.program_id(0) == 0)
    def _():
        copy.start()
        for half in range(2):
            at = pl.ds(half * 128, 128)
            shift_grad[at] = sums[half]
            gain_grad[at] = sums[2 + half]

    for half in range(2):
        v = kg[0, half].astype(F32).reshape(RED * PIECE, 128)
        kgrad[:, pl.ds(half * 128, 128)] = v

    @pl.when(pl.program_id(0) == PARTS - 1)
    def _():
        copy.wait()


def local(features, cotangent, kernel, norm_gain, norm_shift):
    any_spec = pl.BlockSpec(memory_space=pl.ANY)
    vmem = pltpu.VMEM
    dma = pltpu.SemaphoreType.DMA
    features, cotangent, kernel, norm_gain, norm_shift = [
        pltpu.with_memory_space_constraint(v, pltpu.HBM)
        for v in (features, cotangent, kernel.reshape(9, CH, CH), norm_gain, norm_shift)
    ]
    fg, kg, sums = pl.pallas_call(
        main_kernel,
        out_shape=(
            jax.ShapeDtypeStruct((ROWS, COLS, CH), BF16),
            jax.ShapeDtypeStruct((PARTS, 2, RED, PIECE, 128), BF16),
            jax.ShapeDtypeStruct((4, 128), F32),
        ),
        in_specs=[pl.BlockSpec(memory_space=pltpu.HBM)] * 5,
        out_specs=(any_spec,) * 3,
        scratch_shapes=[
            vmem((ROWS, COLS, CH), BF16),
            vmem((ROWS, COLS, CH), BF16),
            vmem((9, CH, CH), BF16),
            vmem((CH,), F32),
            vmem((CH,), F32),
            vmem((ROWS, COLS, CH), BF16),
            vmem((3, 2, CELLS + 16, 128), F32),
            vmem((3, CELLS, CH), BF16),
            vmem((3, CELLS + 16, CH), BF16),
            vmem((3, 128, CH), BF16),
            vmem((CELLS, CH), F32),
            vmem((CH, CELLS), BF16),
            vmem((2, ROWS, CH), BF16),
            vmem((2, ROWS, CH), BF16),
            vmem((2, 3, 8, CH), F32),
            vmem((2, 3, 8, CH), F32),
            vmem((2, 3, 8, CH), F32),
            vmem((4, 128), F32),
            vmem((32, 4, 128), F32),
            vmem((4, 128), F32),
            vmem((16, 4, 128), F32),
            vmem((4, 128), F32),
            vmem((32, 4, 128), F32),
            vmem((4, 128), F32),
            vmem((16, 4, 128), F32),
            vmem((4, 128), F32),
            vmem((PARTS, RED * PIECE, 128), F32),
            vmem((PARTS, RED * PIECE, 128), BF16),
            vmem((PARTS, RED * PIECE, 128), BF16),
            vmem((PARTS, RED, PIECE, 128), BF16),
            vmem((PARTS, RED, PIECE, 128), BF16),
            vmem((PARTS, PIECE, 128), BF16),
            vmem((PARTS, 8, PIECE, 128), BF16),
            vmem((PARTS, RED, PIECE, 128), BF16),
            vmem((PARTS, RED, PIECE, 128), BF16),
            pltpu.SemaphoreType.REGULAR,
            dma((5,)),
            dma((2 * PARTS + 2,)),
            dma((2,)), dma((2,)),
            dma((3,)), dma((3,)),
            dma((4,)), dma((4,)),
            dma((PARTS,)), dma((PARTS,)),
            dma((PARTS,)), dma((PARTS,)),
            dma((PARTS,)), dma((PARTS,)),
            dma((PARTS,)), dma((PARTS,)),
            dma((PARTS,)), dma((PARTS,)),
        ],
        compiler_params=pltpu.CompilerParams(
            collective_id=0, has_side_effects=True, vmem_limit_bytes=48 * 2**20
        ),
        name="backward",
    )(features, cotangent, kernel, norm_gain, norm_shift)
    kgrad, fg, gain_grad, shift_grad = pl.pallas_call(
        last_kernel,
        grid=(PARTS,),
        out_shape=(
            jax.ShapeDtypeStruct((9 * CH, CH), F32),
            jax.ShapeDtypeStruct((ROWS, COLS, CH), BF16),
            jax.ShapeDtypeStruct((CH,), F32),
            jax.ShapeDtypeStruct((CH,), F32),
        ),
        in_specs=[
            pl.BlockSpec((1, 2, RED, PIECE, 128), lambda i: (i, 0, 0, 0, 0)),
            any_spec,
            pl.BlockSpec((4, 128), lambda i: (0, 0)),
        ],
        out_specs=(
            pl.BlockSpec((RED * PIECE, CH), lambda i: (i, 0)),
            any_spec,
            pl.BlockSpec((CH,), lambda i: (0,)),
            pl.BlockSpec((CH,), lambda i: (0,)),
        ),
        scratch_shapes=[dma],
        compiler_params=pltpu.CompilerParams(vmem_limit_bytes=16 * 2**20),
        name="outputs",
    )(kg, fg, sums)
    return fg, kgrad.reshape(3, 3, CH, CH), gain_grad, shift_grad


def solution(mesh):
    placed = (P("lat", "lon", None), P("lat", "lon", None), P(), P(), P())
    return jax.shard_map(
        local,
        mesh=mesh,
        in_specs=placed,
        out_specs=(P("lat", "lon", None), P(), P(), P()),
        check_vma=False,
    )
```

```python
import jax
import jax.numpy as jnp
from jax import lax
from jax.experimental import pallas as pl
from jax.experimental.pallas import tpu as pltpu
from jax.sharding import PartitionSpec as P

MESH = pl.DeviceIdType.MESH
F32 = jnp.float32
BF16 = jnp.bfloat16

GROUP = 8
EPS = 1e-06
CH = 256
ROWS, COLS = 128, 8
CELLS = ROWS * COLS
ALL_CELLS = 512 * 1024
TAPS = ((3, 4, 5), (0, 1, 2), (6, 7, 8))
PARTS = len(TAPS)
RED = 32
PIECES = [len(taps) * CH // RED for taps in TAPS]
BLOCKS = 8
BLOCK = CELLS // BLOCKS


def ring(d, n):
    return min(d, n - d)


PLANE = sorted(
    [(dx, dy, dc) for dx in range(4) for dy in range(4) for dc in range(2)][1:],
    key=lambda d: -(ring(d[0], 4) + ring(d[1], 4) + 0.1 * d[2]),
)
COLUMN = sorted(range(1, 16), key=lambda d: -ring(d, 16))
SLAB = sorted(
    [(dx, dy, dz) for dx in range(4) for dy in range(4) for dz in range(2)][1:],
    key=lambda d: -(ring(d[0], 4) + ring(d[1], 4) + d[2]),
)
EVERY_OTHER = sorted(range(1, 8), key=lambda d: -ring(d, 8))


def device(x, y, z, c):
    return ((x * 16 + z) * 2 + lax.rem(y, 2), lax.div(y, 2) * 2 + c)


def wrapped(a, d, n):
    return lax.rem(a + d, n)


def over_group(v):
    lane = lax.broadcasted_iota(jnp.int32, v.shape, 1)
    for s in (1, 2, 4):
        up = pltpu.roll(v, 128 - s, 1)
        down = pltpu.roll(v, s, 1)
        v = v + jnp.where(lax.rem(lax.div(lane, s), 2) == 0, up, down)
    return v


def row(v):
    return jnp.concatenate([v[0:1], v[1:2]], axis=1)


def main_kernel(*refs):
    refs = list(refs)

    def several(n):
        out = refs[:n]
        del refs[:n]
        return out

    feat_hbm, cot_hbm, w_hbm, gain_hbm, shift_hbm, fg_hbm, sums_hbm = several(7)
    kg_hbm = several(PARTS)
    xv, cv, wv, gv, sv, fgv = several(6)
    stage, even, odd, pole, hg, ht = several(6)
    edge_out, edge_in, rows_out, rows_in, turn_in = several(5)
    pay1, in1, pay2, in2, spay1, sin1, spay2, sin2, sumsv = several(9)
    own, core_out, core_in, cut, cut_in, mid, mid_in, whole = [
        several(PARTS) for _ in range(8)
    ]
    relay_sem, load_sem, out_sem = several(3)
    edge_s, edge_r, rows_s, rows_r, st_s, st_r = several(6)
    core_s, core_r, cut_s, cut_r, mid_s, mid_r = several(6)
    who_s, who_r, oth_s, oth_r = several(4)

    lon = lax.axis_index("lon")
    lat = lax.axis_index("lat")
    x = lax.div(lon, 32)
    z = lax.rem(lax.div(lon, 2), 16)
    y = lax.div(lat, 2) * 2 + lax.rem(lon, 2)
    c = lax.rem(lat, 2)
    zh = lax.div(z, 2)
    zl = lax.rem(z, 2)
    plane_rank = (x * 4 + y) * 2 + c
    slab_rank = (x * 4 + y) * 2 + zl
    at_top = lat == 0
    at_bottom = lat == 3
    east = (wrapped(lon, 1, 128), lat)
    west = (wrapped(lon, 127, 128), lat)
    south = (lon, wrapped(lat, 1, 4))
    north = (lon, wrapped(lat, 3, 4))
    half_turn = (wrapped(lon, 64, 128), lat)
    other_core = (lon, lat + 1 - 2 * c)

    def plane_peers():
        for dx, dy, dc in PLANE:
            yield device(wrapped(x, dx, 4), wrapped(y, dy, 4), z, lax.rem(c + dc, 2))

    def column_peers():
        for dz in COLUMN:
            yield device(x, y, wrapped(z, dz, 16), c)

    def send(src, dst, s, r, to):
        pltpu.make_async_remote_copy(
            src_ref=src, dst_ref=dst, send_sem=s, recv_sem=r,
            device_id=to, device_id_type=MESH,
        ).start()

    def take(ref, sem):
        pltpu.make_async_copy(ref, ref, sem).wait()

    def get(b, start, size):
        at = pl.ds(start, size)
        return jnp.concatenate([stage[b, 0, at, :], stage[b, 1, at, :]], axis=1)

    def put(b, start, v):
        at = pl.ds(start, v.shape[0])
        stage[b, 0, at, :] = v[:, :128]
        stage[b, 1, at, :] = v[:, 128:]

    loads = [
        pltpu.make_async_copy(src, dst, load_sem.at[i])
        for i, (src, dst) in enumerate(
            ((feat_hbm, xv), (cot_hbm, cv), (w_hbm, wv), (gain_hbm, gv), (shift_hbm, sv))
        )
    ]
    loads[0].start()

    barrier = pltpu.get_barrier_semaphore()
    greeted = [device(x, y, wrapped(z, d, 16), c) for d in (4, 12)]
    for dx, dy, dz in SLAB:
        if dz == 1 and (dx, dy) != (0, 0):
            greeted.append(
                device(wrapped(x, dx, 4), wrapped(y, dy, 4), z + 1 - 2 * zl, c)
            )
    greeted += list(plane_peers())
    greeted += [device(x, y, wrapped(z, d, 16), c) for d in (3, 13, 2, 14, 1, 15)]
    greeted += [east, west]
    for peer in greeted:
        pl.semaphore_signal(barrier, inc=1, device_id=peer, device_id_type=MESH)
    for load in loads[1:]:
        load.start()

    loads[0].wait()

    def add_up(i, acc):
        return acc + jnp.sum(xv[pl.ds(i * 16, 16)].astype(F32), axis=0)

    zero = jnp.zeros((COLS, CH), F32)
    total = lax.fori_loop(0, 8, add_up, zero, unroll=True)
    mean = jnp.sum(total, axis=0, keepdims=True) * (1.0 / CELLS)

    def spread(i, acc):
        d = xv[pl.ds(i * 16, 16)].astype(F32) - mean.reshape(1, 1, CH)
        return acc + jnp.sum(d * d, axis=0)

    total = lax.fori_loop(0, 8, spread, zero, unroll=True)
    dev = jnp.sum(total, axis=0, keepdims=True)
    pay1[0:1] = mean[:, :128]
    pay1[1:2] = mean[:, 128:]
    pay1[2:3] = dev[:, :128]
    pay1[3:4] = dev[:, 128:]
    in1[plane_rank] = pay1[...]

    pl.semaphore_wait(barrier, len(greeted))
    for d in (4, 12):
        pl.semaphore_signal(
            relay_sem, inc=1, device_id=device(x, y, wrapped(z, d, 16), c),
            device_id_type=MESH,
        )
    for peer in plane_peers():
        send(pay1, in1.at[plane_rank], st_s.at[0], st_r.at[0], peer)

    loads[1].wait()
    for i in range(BLOCKS):
        put(1, 8 + i * BLOCK, cv[pl.ds(i * 16, 16)].astype(F32).reshape(BLOCK, CH))
    for half in range(2):
        lanes = pl.ds(half * 128, 128)
        for side, col in ((0, 7), (1, 0)):
            v = stage[1, half, pl.ds(8 + col, ROWS, stride=8), :]
            edge_out[side, :, lanes] = v.astype(BF16)

    take(in1.at[pl.ds(0, 31)], st_r.at[0])
    v = in1[...]
    total = jnp.sum(v, axis=0)
    avg = total * (1.0 / 32)
    d = v - avg[None]
    sq = jnp.sum(d * d, axis=0)
    pay2[0:2] = avg[0:2]
    pay2[2:4] = total[2:4] + float(CELLS) * sq[0:2]
    in2[z] = pay2[...]
    pl.semaphore_wait(relay_sem, 2)
    for peer in column_peers():
        send(pay2, in2.at[z], st_s.at[1], st_r.at[1], peer)
    send(edge_out.at[0], edge_in.at[0], edge_s.at[0], edge_r.at[0], east)
    send(edge_out.at[1], edge_in.at[1], edge_s.at[1], edge_r.at[1], west)

    for i in range(BLOCKS):
        lo = 8 + i * BLOCK
        v = get(1, lo, BLOCK)
        even[1, pl.ds(i * BLOCK, BLOCK), :] = v.astype(BF16)
        put(2, lo, pltpu.roll(v, 1, 0))
        put(0, lo, pltpu.roll(v, BLOCK - 1, 0))
    take(edge_in.at[0], edge_r.at[0])
    take(edge_in.at[1], edge_r.at[1])
    for half in range(2):
        lanes = pl.ds(half * 128, 128)
        for b, side, col in ((2, 0, 0), (0, 1, 7)):
            v = edge_in[side, :, lanes].astype(F32)
            stage[b, half, pl.ds(8 + col, ROWS, stride=8), :] = v
    for b in range(3):
        rows_out[0, b] = get(b, 8, 8)
        rows_out[1, b] = get(b, CELLS, 8)
    send(rows_out.at[0], rows_in.at[1], rows_s.at[0], rows_r.at[0], north)
    send(rows_out.at[1], rows_in.at[0], rows_s.at[1], rows_r.at[1], south)
    send(rows_out, turn_in, rows_s.at[2], rows_r.at[2], half_turn)
    for b in (0, 2):
        even[b] = get(b, 8, CELLS).astype(BF16)

    def window(a, b, start, size):
        if a == 0:
            return odd[b, pl.ds(16 + start, size), :]
        if a == 1:
            return even[b, pl.ds(start, size), :]
        return odd[b, pl.ds(start, size), :]

    loads[3].wait()
    loads[4].wait()
    take(in2.at[pl.ds(0, 15)], st_r.at[1])
    v = in2[...]
    total = jnp.sum(v, axis=0)
    avg = total * (1.0 / 16)
    d = v - avg[None]
    sq = jnp.sum(d * d, axis=0)
    ch_mean = avg[0:2]
    ch_dev = total[2:4] + float(CELLS * 32) * sq[0:2]
    g_mean = over_group(ch_mean) * (1.0 / GROUP)
    off = ch_mean - g_mean
    g_var = over_group(ch_dev + float(ALL_CELLS) * off * off) * (
        1.0 / (GROUP * ALL_CELLS)
    )
    inv = row(1.0 / jnp.sqrt(g_var + EPS))
    mean = row(g_mean)
    gain = gv[...].reshape(1, CH)
    shift = sv[...].reshape(1, CH)

    def standard(i):
        return (xv[pl.ds(i * 16, 16)].astype(F32).reshape(BLOCK, CH) - mean) * inv

    def logistic(v):
        d = 1.0 + jnp.exp(jnp.minimum(-v, 87.0))
        r = pl.reciprocal(d, approx=True)
        return r * (2.0 - d * r)

    for i in range(BLOCKS):
        at = pl.ds(i * BLOCK, BLOCK)
        nm = standard(i) * gain + shift
        h = (nm * logistic(nm)).astype(BF16)
        ht[:, at] = h.T
        if i == 0:
            first = h[0:16]
        if i == BLOCKS - 1:
            last = h[BLOCK - 16 : BLOCK]
    keep = lax.broadcasted_iota(jnp.int32, (128, CH), 0)
    zeros = jnp.zeros((112, CH), BF16)
    first = jnp.concatenate([first, zeros], axis=0).astype(F32)
    last = jnp.concatenate([last, zeros], axis=0).astype(F32)
    first_t = jnp.where(keep < 8, first, 0.0).astype(BF16).T
    last_t = jnp.where((keep >= 8) & (keep < 16), last, 0.0).astype(BF16).T

    def partial(p):
        for k, tap in enumerate(TAPS[p]):
            a, b = tap // 3, tap % 3
            r = jnp.dot(ht[...], window(a, b, 0, CELLS), preferred_element_type=F32)
            if a == 0:
                r = r + jnp.dot(first_t, pole[b], preferred_element_type=F32)
            if a == 2:
                r = r + jnp.dot(last_t, pole[b], preferred_element_type=F32)
            at = pl.ds(k * CH, CH)
            own[p][at, :] = jnp.where(c == 0, r[:, :128], r[:, 128:])
            core_out[p][at, :] = jnp.where(c == 0, r[:, 128:], r[:, :128]).astype(BF16)
        send(core_out[p], core_in[p], core_s.at[p], core_r.at[p], other_core)

    def scatter(p):
        take(core_in[p], core_r.at[p])
        v = own[p][...] + core_in[p][...].astype(F32)
        cut[p][...] = v.reshape(RED, PIECES[p], 128).astype(BF16)
        cut_in[p][slab_rank] = cut[p][slab_rank]
        for dx, dy, dz in SLAB:
            px, py = wrapped(x, dx, 4), wrapped(y, dy, 4)
            pz = lax.rem(zl + dz, 2)
            rank = (px * 4 + py) * 2 + pz
            send(
                cut[p].at[rank], cut_in[p].at[slab_rank], cut_s.at[p], cut_r.at[p],
                device(px, py, zh * 2 + pz, c),
            )

    def exchange(p):
        take(cut_in[p].at[pl.ds(0, RED - 1)], cut_r.at[p])
        v = jnp.sum(cut_in[p][...].astype(F32), axis=0).astype(BF16)
        mid[p][...] = v
        mid_in[p][zh] = v
        for d in EVERY_OTHER:
            send(
                mid[p], mid_in[p].at[zh], mid_s.at[p], mid_r.at[p],
                device(x, y, wrapped(zh, d, 8) * 2 + zl, c),
            )

    def gather(p):
        take(mid_in[p].at[pl.ds(0, 7)], mid_r.at[p])
        v = jnp.sum(mid_in[p][...].astype(F32), axis=0) * (1.0 / ALL_CELLS)
        whole[p][slab_rank] = v.astype(BF16)
        mine = whole[p].at[slab_rank]
        for dx, dy, dz in SLAB:
            px, py = wrapped(x, dx, 4), wrapped(y, dy, 4)
            send(
                mine, mine, who_s.at[p], who_r.at[p],
                device(px, py, zh * 2 + lax.rem(zl + dz, 2), c),
            )

    def keep_own(p):
        return pltpu.make_async_copy(whole[p], kg_hbm[p].at[c], out_sem.at[p])

    def hand_over(p):
        take(whole[p].at[pl.ds(0, RED - 1)], who_r.at[p])
        send(whole[p], kg_hbm[p].at[c], oth_s.at[p], oth_r.at[p], other_core)
        keep_own(p).start()

    def rows_arrive():
        pole[...] = jnp.zeros_like(pole)
        take(rows_in.at[1], rows_r.at[0])
        take(rows_in.at[0], rows_r.at[1])
        take(turn_in, rows_r.at[2])
        for b in range(3):
            put(b, 0, jnp.where(at_top, 0.0, rows_in[0, b]))
            put(b, 8 + CELLS, jnp.where(at_bottom, 0.0, rows_in[1, b]))
            odd[b] = get(b, 0, CELLS + 16).astype(BF16)
            pole[b, pl.ds(0, 16), :] = jnp.concatenate(
                [
                    jnp.where(at_top, turn_in[0, b], 0.0),
                    jnp.where(at_bottom, turn_in[1, b], 0.0),
                ],
                axis=0,
            ).astype(BF16)

    partial(0)
    scatter(0)
    rows_arrive()
    partial(1)
    partial(2)
    scatter(1)
    scatter(2)

    loads[2].wait()
    contract_last = (((1,), (1,)), ((), ()))
    for i in range(4):
        acc = None
        for a in range(3):
            for b in range(3):
                part = lax.dot_general(
                    window(a, b, i * 256, 256), wv[a * 3 + b], contract_last,
                    preferred_element_type=F32,
                )
                acc = part if acc is None else acc + part
        hg[pl.ds(i * 256, 256), :] = acc
    for a, at in ((0, 0), (2, 1)):
        acc = None
        for b in range(3):
            part = lax.dot_general(
                pole[b, pl.ds(0, 16), :], wv[a * 3 + b], contract_last,
                preferred_element_type=F32,
            )
            acc = part if acc is None else acc + part
        where = pl.ds(0, 8) if at == 0 else pl.ds(CELLS - 8, 8)
        hg[where, :] = hg[where, :] + acc[at * 8 : at * 8 + 8]

    acc1 = zero
    acc2 = zero
    for i in range(BLOCKS):
        at = pl.ds(i * BLOCK, BLOCK)
        s0 = standard(i)
        nm = s0 * gain + shift
        s = logistic(nm)
        ng = hg[at, :] * (s * (1.0 + nm * (1.0 - s)))
        hg[at, :] = ng
        acc1 = acc1 + jnp.sum(ng.reshape(16, 8, CH), axis=0)
        acc2 = acc2 + jnp.sum((ng * s0).reshape(16, 8, CH), axis=0)
    s1 = jnp.sum(acc1, axis=0, keepdims=True)
    s2 = jnp.sum(acc2, axis=0, keepdims=True)
    spay1[0:1] = s1[:, :128]
    spay1[1:2] = s1[:, 128:]
    spay1[2:3] = s2[:, :128]
    spay1[3:4] = s2[:, 128:]
    sin1[plane_rank] = spay1[...]
    for peer in plane_peers():
        send(spay1, sin1.at[plane_rank], st_s.at[2], st_r.at[2], peer)

    for p in range(PARTS):
        exchange(p)
    take(sin1.at[pl.ds(0, 31)], st_r.at[2])
    spay2[...] = jnp.sum(sin1[...], axis=0)
    sin2[z] = spay2[...]
    for peer in column_peers():
        send(spay2, sin2.at[z], st_s.at[3], st_r.at[3], peer)
    for p in range(PARTS):
        gather(p)

    take(sin2.at[pl.ds(0, 15)], st_r.at[3])
    grads = jnp.sum(sin2[...], axis=0) * (1.0 / ALL_CELLS)
    sumsv[...] = grads
    to_sums = pltpu.make_async_copy(sumsv, sums_hbm, out_sem.at[PARTS])
    to_sums.start()
    gain2 = jnp.concatenate([gain[:, :128], gain[:, 128:]], axis=0)
    m1 = row(over_group(gain2 * grads[0:2]) * (1.0 / GROUP))
    m2 = row(over_group(gain2 * grads[2:4]) * (1.0 / GROUP))
    for i in range(BLOCKS):
        at = pl.ds(i * BLOCK, BLOCK)
        v = inv * (hg[at, :] * gain - m1 - standard(i) * m2)
        fgv[pl.ds(i * 16, 16)] = v.reshape(16, 8, CH).astype(BF16)
    to_fg = pltpu.make_async_copy(fgv, fg_hbm, out_sem.at[PARTS + 1])
    to_fg.start()

    for p in range(PARTS):
        hand_over(p)

    take(edge_out.at[0], edge_s.at[0])
    take(edge_out.at[1], edge_s.at[1])
    take(rows_out.at[0], rows_s.at[0])
    take(rows_out.at[1], rows_s.at[1])
    take(rows_out, rows_s.at[2])
    take(in1.at[pl.ds(0, 31)], st_s.at[0])
    take(in2.at[pl.ds(0, 15)], st_s.at[1])
    take(sin1.at[pl.ds(0, 31)], st_s.at[2])
    take(sin2.at[pl.ds(0, 15)], st_s.at[3])
    for p in range(PARTS):
        take(core_out[p], core_s.at[p])
        take(cut[p].at[pl.ds(0, RED - 1)], cut_s.at[p])
        take(mid_in[p].at[pl.ds(0, 7)], mid_s.at[p])
        take(whole[p].at[pl.ds(0, RED - 1)], who_s.at[p])
    to_sums.wait()
    to_fg.wait()
    for p in range(PARTS):
        take(whole[p], oth_s.at[p])
        keep_own(p).wait()
        take(kg_hbm[p].at[1 - c], oth_r.at[p])


def last_kernel(*refs):
    kg = refs[:PARTS]
    fg, sums, kgrad, fg_out, gain_grad, shift_grad, wide, flat, sem = refs[PARTS:]
    outs = [pltpu.make_async_copy(fg, fg_out, sem.at[9])]
    outs[0].start()
    for i, out in ((0, shift_grad), (1, gain_grad)):
        for half in range(2):
            flat[i, pl.ds(half * 128, 128)] = sums[2 * i + half]
        outs.append(pltpu.make_async_copy(flat.at[i], out, sem.at[10 + i]))
        outs[-1].start()
    for p in range(PARTS):
        for k, tap in enumerate(TAPS[p]):
            at = pl.ds(tap * CH, CH)
            for half in range(2):
                v = kg[p][half].astype(F32).reshape(RED * PIECES[p], 128)
                wide[at, pl.ds(half * 128, 128)] = v[k * CH : (k + 1) * CH]
            outs.append(pltpu.make_async_copy(wide.at[at], kgrad.at[at], sem.at[tap]))
            outs[-1].start()
    for out in outs:
        out.wait()


def local(features, cotangent, kernel, norm_gain, norm_shift):
    any_spec = pl.BlockSpec(memory_space=pl.ANY)
    vmem = pltpu.VMEM
    dma = pltpu.SemaphoreType.DMA
    features, cotangent, kernel, norm_gain, norm_shift = [
        pltpu.with_memory_space_constraint(v, pltpu.HBM)
        for v in (features, cotangent, kernel.reshape(9, CH, CH), norm_gain, norm_shift)
    ]
    rows = [RED * piece for piece in PIECES]
    shared = [(RED, piece, 128) for piece in PIECES]
    fg, sums, *kg = pl.pallas_call(
        main_kernel,
        out_shape=[
            jax.ShapeDtypeStruct((ROWS, COLS, CH), BF16),
            jax.ShapeDtypeStruct((4, 128), F32),
        ]
        + [jax.ShapeDtypeStruct((2,) + shape, BF16) for shape in shared],
        in_specs=[pl.BlockSpec(memory_space=pltpu.HBM)] * 5,
        out_specs=[any_spec] * (2 + PARTS),
        scratch_shapes=[
            vmem((ROWS, COLS, CH), BF16),
            vmem((ROWS, COLS, CH), BF16),
            vmem((9, CH, CH), BF16),
            vmem((CH,), F32),
            vmem((CH,), F32),
            vmem((ROWS, COLS, CH), BF16),
            vmem((3, 2, CELLS + 16, 128), F32),
            vmem((3, CELLS, CH), BF16),
            vmem((3, CELLS + 16, CH), BF16),
            vmem((3, 128, CH), BF16),
            vmem((CELLS, CH), F32),
            vmem((CH, CELLS), BF16),
            vmem((2, ROWS, CH), BF16),
            vmem((2, ROWS, CH), BF16),
            vmem((2, 3, 8, CH), F32),
            vmem((2, 3, 8, CH), F32),
            vmem((2, 3, 8, CH), F32),
            vmem((4, 128), F32),
            vmem((32, 4, 128), F32),
            vmem((4, 128), F32),
            vmem((16, 4, 128), F32),
            vmem((4, 128), F32),
            vmem((32, 4, 128), F32),
            vmem((4, 128), F32),
            vmem((16, 4, 128), F32),
            vmem((4, 128), F32),
            *[vmem((n, 128), F32) for n in rows],
            *[vmem((n, 128), BF16) for n in rows],
            *[vmem((n, 128), BF16) for n in rows],
            *[vmem(shape, BF16) for shape in shared],
            *[vmem(shape, BF16) for shape in shared],
            *[vmem((piece, 128), BF16) for piece in PIECES],
            *[vmem((8, piece, 128), BF16) for piece in PIECES],
            *[vmem(shape, BF16) for shape in shared],
            pltpu.SemaphoreType.REGULAR,
            dma((5,)),
            dma((PARTS + 2,)),
            dma((2,)), dma((2,)),
            dma((3,)), dma((3,)),
            dma((4,)), dma((4,)),
            dma((PARTS,)), dma((PARTS,)),
            dma((PARTS,)), dma((PARTS,)),
            dma((PARTS,)), dma((PARTS,)),
            dma((PARTS,)), dma((PARTS,)),
            dma((PARTS,)), dma((PARTS,)),
        ],
        compiler_params=pltpu.CompilerParams(
            collective_id=0, has_side_effects=True, vmem_limit_bytes=48 * 2**20
        ),
        name="backward",
    )(features, cotangent, kernel, norm_gain, norm_shift)
    in_vmem = pl.BlockSpec(memory_space=pltpu.VMEM)
    kgrad, fg, gain_grad, shift_grad = pl.pallas_call(
        last_kernel,
        out_shape=(
            jax.ShapeDtypeStruct((9 * CH, CH), F32),
            jax.ShapeDtypeStruct((ROWS, COLS, CH), BF16),
            jax.ShapeDtypeStruct((CH,), F32),
            jax.ShapeDtypeStruct((CH,), F32),
        ),
        in_specs=[in_vmem] * (PARTS + 2),
        out_specs=(any_spec,) * 4,
        scratch_shapes=[vmem((9 * CH, CH), F32), vmem((2, CH), F32), dma((12,))],
        compiler_params=pltpu.CompilerParams(vmem_limit_bytes=16 * 2**20),
        name="outputs",
    )(*kg, fg, sums)
    return fg, kgrad.reshape(3, 3, CH, CH), gain_grad, shift_grad


def solution(mesh):
    placed = (P("lat", "lon", None), P("lat", "lon", None), P(), P(), P())
    return jax.shard_map(
        local,
        mesh=mesh,
        in_specs=placed,
        out_specs=(P("lat", "lon", None), P(), P(), P()),
        check_vma=False,
    )
```

```python
import jax
import jax.numpy as jnp
from jax import lax
from jax.experimental import pallas as pl
from jax.experimental.pallas import tpu as pltpu
from jax.sharding import PartitionSpec as P

MESH = pl.DeviceIdType.MESH
F32 = jnp.float32
BF16 = jnp.bfloat16

GROUP = 8
EPS = 1e-06
CH = 256
ROWS, COLS = 128, 8
CELLS = ROWS * COLS
ALL_CELLS = 512 * 1024
TAPS = ((3, 4, 5), (0, 1, 2), (6, 7, 8))
PARTS = len(TAPS)
RED = 32
PIECES = [len(taps) * CH // RED for taps in TAPS]
BLOCKS = 8
BLOCK = CELLS // BLOCKS


def ring(d, n):
    return min(d, n - d)


PLANE = sorted(
    [(dx, dy, dc) for dx in range(4) for dy in range(4) for dc in range(2)][1:],
    key=lambda d: -(ring(d[0], 4) + ring(d[1], 4) + 0.1 * d[2]),
)
COLUMN = sorted(range(1, 16), key=lambda d: -ring(d, 16))
SLAB = sorted(
    [(dx, dy, dz) for dx in range(4) for dy in range(4) for dz in range(2)][1:],
    key=lambda d: -(ring(d[0], 4) + ring(d[1], 4) + d[2]),
)
EVERY_OTHER = sorted(range(1, 8), key=lambda d: -ring(d, 8))


def device(x, y, z, c):
    return ((x * 16 + z) * 2 + lax.rem(y, 2), lax.div(y, 2) * 2 + c)


def wrapped(a, d, n):
    return lax.rem(a + d, n)


def over_group(v):
    lane = lax.broadcasted_iota(jnp.int32, v.shape, 1)
    for s in (1, 2, 4):
        up = pltpu.roll(v, 128 - s, 1)
        down = pltpu.roll(v, s, 1)
        v = v + jnp.where(lax.rem(lax.div(lane, s), 2) == 0, up, down)
    return v


def row(v):
    return jnp.concatenate([v[0:1], v[1:2]], axis=1)


def main_kernel(*refs):
    refs = list(refs)

    def several(n):
        out = refs[:n]
        del refs[:n]
        return out

    feat_hbm, cot_hbm, w_hbm, gain_hbm, shift_hbm, fg_hbm, sums_hbm = several(7)
    kg_hbm = several(PARTS)
    xv, cv, wv, gv, sv, fgv = several(6)
    stage, even, odd, pole, hg, ht = several(6)
    edge_out, edge_in, rows_out, rows_in, turn_in = several(5)
    pay1, in1, pay2, in2, spay1, sin1, spay2, sin2, sumsv = several(9)
    own, core_out, core_in, cut, cut_in, mid, mid_in, whole = [
        several(PARTS) for _ in range(8)
    ]
    relay_sem, load_sem, out_sem = several(3)
    edge_s, edge_r, rows_s, rows_r, st_s, st_r = several(6)
    core_s, core_r, cut_s, cut_r, mid_s, mid_r = several(6)
    who_s, who_r, oth_s, oth_r = several(4)

    lon = lax.axis_index("lon")
    lat = lax.axis_index("lat")
    x = lax.div(lon, 32)
    z = lax.rem(lax.div(lon, 2), 16)
    y = lax.div(lat, 2) * 2 + lax.rem(lon, 2)
    c = lax.rem(lat, 2)
    zh = lax.div(z, 2)
    zl = lax.rem(z, 2)
    plane_rank = (x * 4 + y) * 2 + c
    slab_rank = (x * 4 + y) * 2 + zl
    at_top = lat == 0
    at_bottom = lat == 3
    east = (wrapped(lon, 1, 128), lat)
    west = (wrapped(lon, 127, 128), lat)
    south = (lon, wrapped(lat, 1, 4))
    north = (lon, wrapped(lat, 3, 4))
    half_turn = (wrapped(lon, 64, 128), lat)
    other_core = (lon, lat + 1 - 2 * c)

    def plane_peers():
        for dx, dy, dc in PLANE:
            yield device(wrapped(x, dx, 4), wrapped(y, dy, 4), z, lax.rem(c + dc, 2))

    def column_peers():
        for dz in COLUMN:
            yield device(x, y, wrapped(z, dz, 16), c)

    def send(src, dst, s, r, to):
        pltpu.make_async_remote_copy(
            src_ref=src, dst_ref=dst, send_sem=s, recv_sem=r,
            device_id=to, device_id_type=MESH,
        ).start()

    def take(ref, sem):
        pltpu.make_async_copy(ref, ref, sem).wait()

    def get(b, start, size):
        at = pl.ds(start, size)
        return jnp.concatenate([stage[b, 0, at, :], stage[b, 1, at, :]], axis=1)

    def put(b, start, v):
        at = pl.ds(start, v.shape[0])
        stage[b, 0, at, :] = v[:, :128]
        stage[b, 1, at, :] = v[:, 128:]

    loads = [
        pltpu.make_async_copy(src, dst, load_sem.at[i])
        for i, (src, dst) in enumerate(
            ((feat_hbm, xv), (cot_hbm, cv), (w_hbm, wv), (gain_hbm, gv), (shift_hbm, sv))
        )
    ]
    loads[0].start()

    barrier = pltpu.get_barrier_semaphore()
    greeted = [device(x, y, wrapped(z, d, 16), c) for d in (4, 12)]
    for dx, dy, dz in SLAB:
        if dz == 1 and (dx, dy) != (0, 0):
            greeted.append(
                device(wrapped(x, dx, 4), wrapped(y, dy, 4), z + 1 - 2 * zl, c)
            )
    greeted += list(plane_peers())
    greeted += [device(x, y, wrapped(z, d, 16), c) for d in (3, 13, 2, 14, 1, 15)]
    greeted += [east, west]
    for peer in greeted:
        pl.semaphore_signal(barrier, inc=1, device_id=peer, device_id_type=MESH)
    for load in loads[1:]:
        load.start()

    loads[0].wait()

    def add_up(i, acc):
        return acc + jnp.sum(xv[pl.ds(i * 16, 16)].astype(F32), axis=0)

    zero = jnp.zeros((COLS, CH), F32)
    total = lax.fori_loop(0, 8, add_up, zero, unroll=True)
    mean = jnp.sum(total, axis=0, keepdims=True) * (1.0 / CELLS)

    def spread(i, acc):
        d = xv[pl.ds(i * 16, 16)].astype(F32) - mean.reshape(1, 1, CH)
        return acc + jnp.sum(d * d, axis=0)

    total = lax.fori_loop(0, 8, spread, zero, unroll=True)
    dev = jnp.sum(total, axis=0, keepdims=True)
    pay1[0:1] = mean[:, :128]
    pay1[1:2] = mean[:, 128:]
    pay1[2:3] = dev[:, :128]
    pay1[3:4] = dev[:, 128:]
    in1[plane_rank] = pay1[...]

    pl.semaphore_wait(barrier, len(greeted))
    for d in (4, 12):
        pl.semaphore_signal(
            relay_sem, inc=1, device_id=device(x, y, wrapped(z, d, 16), c),
            device_id_type=MESH,
        )
    for peer in plane_peers():
        send(pay1, in1.at[plane_rank], st_s.at[0], st_r.at[0], peer)

    loads[1].wait()
    for i in range(BLOCKS):
        put(1, 8 + i * BLOCK, cv[pl.ds(i * 16, 16)].astype(F32).reshape(BLOCK, CH))
    for half in range(2):
        lanes = pl.ds(half * 128, 128)
        for side, col in ((0, 7), (1, 0)):
            v = stage[1, half, pl.ds(8 + col, ROWS, stride=8), :]
            edge_out[side, :, lanes] = v.astype(BF16)

    take(in1.at[pl.ds(0, 31)], st_r.at[0])
    v = in1[...]
    total = jnp.sum(v, axis=0)
    avg = total * (1.0 / 32)
    d = v - avg[None]
    sq = jnp.sum(d * d, axis=0)
    pay2[0:2] = avg[0:2]
    pay2[2:4] = total[2:4] + float(CELLS) * sq[0:2]
    in2[z] = pay2[...]
    pl.semaphore_wait(relay_sem, 2)
    for peer in column_peers():
        send(pay2, in2.at[z], st_s.at[1], st_r.at[1], peer)
    send(edge_out.at[0], edge_in.at[0], edge_s.at[0], edge_r.at[0], east)
    send(edge_out.at[1], edge_in.at[1], edge_s.at[1], edge_r.at[1], west)

    for i in range(BLOCKS):
        lo = 8 + i * BLOCK
        v = get(1, lo, BLOCK)
        even[1, pl.ds(i * BLOCK, BLOCK), :] = v.astype(BF16)
        put(2, lo, pltpu.roll(v, 1, 0))
        put(0, lo, pltpu.roll(v, BLOCK - 1, 0))
    take(edge_in.at[0], edge_r.at[0])
    take(edge_in.at[1], edge_r.at[1])
    for half in range(2):
        lanes = pl.ds(half * 128, 128)
        for b, side, col in ((2, 0, 0), (0, 1, 7)):
            v = edge_in[side, :, lanes].astype(F32)
            stage[b, half, pl.ds(8 + col, ROWS, stride=8), :] = v
    for b in range(3):
        rows_out[0, b] = get(b, 8, 8)
        rows_out[1, b] = get(b, CELLS, 8)
    send(rows_out.at[0], rows_in.at[1], rows_s.at[0], rows_r.at[0], north)
    send(rows_out.at[1], rows_in.at[0], rows_s.at[1], rows_r.at[1], south)
    send(rows_out, turn_in, rows_s.at[2], rows_r.at[2], half_turn)
    for b in (0, 2):
        even[b] = get(b, 8, CELLS).astype(BF16)

    def window(a, b, start, size):
        if a == 0:
            return odd[b, pl.ds(16 + start, size), :]
        if a == 1:
            return even[b, pl.ds(start, size), :]
        return odd[b, pl.ds(start, size), :]

    loads[3].wait()
    loads[4].wait()
    take(in2.at[pl.ds(0, 15)], st_r.at[1])
    v = in2[...]
    total = jnp.sum(v, axis=0)
    avg = total * (1.0 / 16)
    d = v - avg[None]
    sq = jnp.sum(d * d, axis=0)
    ch_mean = avg[0:2]
    ch_dev = total[2:4] + float(CELLS * 32) * sq[0:2]
    g_mean = over_group(ch_mean) * (1.0 / GROUP)
    off = ch_mean - g_mean
    g_var = over_group(ch_dev + float(ALL_CELLS) * off * off) * (
        1.0 / (GROUP * ALL_CELLS)
    )
    inv = row(1.0 / jnp.sqrt(g_var + EPS))
    mean = row(g_mean)
    gain = gv[...].reshape(1, CH)
    shift = sv[...].reshape(1, CH)

    def standard(i):
        return (xv[pl.ds(i * 16, 16)].astype(F32).reshape(BLOCK, CH) - mean) * inv

    def logistic(v):
        d = 1.0 + jnp.exp(jnp.minimum(-v, 87.0))
        r = pl.reciprocal(d, approx=True)
        return r * (2.0 - d * r)

    for i in range(BLOCKS):
        at = pl.ds(i * BLOCK, BLOCK)
        nm = standard(i) * gain + shift
        h = (nm * logistic(nm)).astype(BF16)
        ht[:, at] = h.T
        if i == 0:
            first = h[0:16]
        if i == BLOCKS - 1:
            last = h[BLOCK - 16 : BLOCK]
    keep = lax.broadcasted_iota(jnp.int32, (128, CH), 0)
    zeros = jnp.zeros((112, CH), BF16)
    first = jnp.concatenate([first, zeros], axis=0).astype(F32)
    last = jnp.concatenate([last, zeros], axis=0).astype(F32)
    first_t = jnp.where(keep < 8, first, 0.0).astype(BF16).T
    last_t = jnp.where((keep >= 8) & (keep < 16), last, 0.0).astype(BF16).T

    def partial(p):
        for k, tap in enumerate(TAPS[p]):
            a, b = tap // 3, tap % 3
            r = jnp.dot(ht[...], window(a, b, 0, CELLS), preferred_element_type=F32)
            if a == 0:
                r = r + jnp.dot(first_t, pole[b], preferred_element_type=F32)
            if a == 2:
                r = r + jnp.dot(last_t, pole[b], preferred_element_type=F32)
            at = pl.ds(k * CH, CH)
            own[p][at, :] = jnp.where(c == 0, r[:, :128], r[:, 128:])
            core_out[p][at, :] = jnp.where(c == 0, r[:, 128:], r[:, :128]).astype(BF16)
        send(core_out[p], core_in[p], core_s.at[p], core_r.at[p], other_core)

    def scatter(p):
        take(core_in[p], core_r.at[p])
        v = own[p][...] + core_in[p][...].astype(F32)
        cut[p][...] = v.reshape(RED, PIECES[p], 128).astype(BF16)
        cut_in[p][slab_rank] = cut[p][slab_rank]
        for dx, dy, dz in SLAB:
            px, py = wrapped(x, dx, 4), wrapped(y, dy, 4)
            pz = lax.rem(zl + dz, 2)
            rank = (px * 4 + py) * 2 + pz
            send(
                cut[p].at[rank], cut_in[p].at[slab_rank], cut_s.at[p], cut_r.at[p],
                device(px, py, zh * 2 + pz, c),
            )

    def exchange(p):
        take(cut_in[p].at[pl.ds(0, RED - 1)], cut_r.at[p])
        v = jnp.sum(cut_in[p][...].astype(F32), axis=0).astype(BF16)
        mid[p][...] = v
        mid_in[p][zh] = v
        for d in EVERY_OTHER:
            send(
                mid[p], mid_in[p].at[zh], mid_s.at[p], mid_r.at[p],
                device(x, y, wrapped(zh, d, 8) * 2 + zl, c),
            )

    def gather(p):
        take(mid_in[p].at[pl.ds(0, 7)], mid_r.at[p])
        v = jnp.sum(mid_in[p][...].astype(F32), axis=0) * (1.0 / ALL_CELLS)
        whole[p][slab_rank] = v.astype(BF16)
        mine = whole[p].at[slab_rank]
        for dx, dy, dz in SLAB:
            px, py = wrapped(x, dx, 4), wrapped(y, dy, 4)
            send(
                mine, mine, who_s.at[p], who_r.at[p],
                device(px, py, zh * 2 + lax.rem(zl + dz, 2), c),
            )

    def keep_own(p):
        return pltpu.make_async_copy(whole[p], kg_hbm[p].at[c], out_sem.at[p])

    def hand_over(p):
        take(whole[p].at[pl.ds(0, RED - 1)], who_r.at[p])
        send(whole[p], kg_hbm[p].at[c], oth_s.at[p], oth_r.at[p], other_core)
        keep_own(p).start()

    def rows_arrive():
        pole[...] = jnp.zeros_like(pole)
        take(rows_in.at[1], rows_r.at[0])
        take(rows_in.at[0], rows_r.at[1])
        take(turn_in, rows_r.at[2])
        for b in range(3):
            put(b, 0, jnp.where(at_top, 0.0, rows_in[0, b]))
            put(b, 8 + CELLS, jnp.where(at_bottom, 0.0, rows_in[1, b]))
            odd[b] = get(b, 0, CELLS + 16).astype(BF16)
            pole[b, pl.ds(0, 16), :] = jnp.concatenate(
                [
                    jnp.where(at_top, turn_in[0, b], 0.0),
                    jnp.where(at_bottom, turn_in[1, b], 0.0),
                ],
                axis=0,
            ).astype(BF16)

    partial(0)
    scatter(0)
    rows_arrive()
    partial(1)
    partial(2)
    scatter(1)
    scatter(2)

    loads[2].wait()
    contract_last = (((1,), (1,)), ((), ()))
    for i in range(4):
        acc = None
        for a in range(3):
            for b in range(3):
                part = lax.dot_general(
                    window(a, b, i * 256, 256), wv[a * 3 + b], contract_last,
                    preferred_element_type=F32,
                )
                acc = part if acc is None else acc + part
        hg[pl.ds(i * 256, 256), :] = acc
    for a, at in ((0, 0), (2, 1)):
        acc = None
        for b in range(3):
            part = lax.dot_general(
                pole[b, pl.ds(0, 16), :], wv[a * 3 + b], contract_last,
                preferred_element_type=F32,
            )
            acc = part if acc is None else acc + part
        where = pl.ds(0, 8) if at == 0 else pl.ds(CELLS - 8, 8)
        hg[where, :] = hg[where, :] + acc[at * 8 : at * 8 + 8]

    acc1 = zero
    acc2 = zero
    for i in range(BLOCKS):
        at = pl.ds(i * BLOCK, BLOCK)
        s0 = standard(i)
        nm = s0 * gain + shift
        s = logistic(nm)
        ng = hg[at, :] * (s * (1.0 + nm * (1.0 - s)))
        hg[at, :] = ng
        acc1 = acc1 + jnp.sum(ng.reshape(16, 8, CH), axis=0)
        acc2 = acc2 + jnp.sum((ng * s0).reshape(16, 8, CH), axis=0)
    s1 = jnp.sum(acc1, axis=0, keepdims=True)
    s2 = jnp.sum(acc2, axis=0, keepdims=True)
    spay1[0:1] = s1[:, :128]
    spay1[1:2] = s1[:, 128:]
    spay1[2:3] = s2[:, :128]
    spay1[3:4] = s2[:, 128:]
    sin1[plane_rank] = spay1[...]
    for peer in plane_peers():
        send(spay1, sin1.at[plane_rank], st_s.at[2], st_r.at[2], peer)

    for p in range(PARTS):
        exchange(p)
    take(sin1.at[pl.ds(0, 31)], st_r.at[2])
    spay2[...] = jnp.sum(sin1[...], axis=0)
    sin2[z] = spay2[...]
    for peer in column_peers():
        send(spay2, sin2.at[z], st_s.at[3], st_r.at[3], peer)
    for p in range(PARTS):
        gather(p)

    for p in range(PARTS):
        hand_over(p)

    take(sin2.at[pl.ds(0, 15)], st_r.at[3])
    grads = jnp.sum(sin2[...], axis=0) * (1.0 / ALL_CELLS)
    sumsv[...] = grads
    to_sums = pltpu.make_async_copy(sumsv, sums_hbm, out_sem.at[PARTS])
    to_sums.start()
    gain2 = jnp.concatenate([gain[:, :128], gain[:, 128:]], axis=0)
    m1 = row(over_group(gain2 * grads[0:2]) * (1.0 / GROUP))
    m2 = row(over_group(gain2 * grads[2:4]) * (1.0 / GROUP))
    for i in range(BLOCKS):
        at = pl.ds(i * BLOCK, BLOCK)
        v = inv * (hg[at, :] * gain - m1 - standard(i) * m2)
        fgv[pl.ds(i * 16, 16)] = v.reshape(16, 8, CH).astype(BF16)
    to_fg = pltpu.make_async_copy(fgv, fg_hbm, out_sem.at[PARTS + 1])
    to_fg.start()

    take(edge_out.at[0], edge_s.at[0])
    take(edge_out.at[1], edge_s.at[1])
    take(rows_out.at[0], rows_s.at[0])
    take(rows_out.at[1], rows_s.at[1])
    take(rows_out, rows_s.at[2])
    take(in1.at[pl.ds(0, 31)], st_s.at[0])
    take(in2.at[pl.ds(0, 15)], st_s.at[1])
    take(sin1.at[pl.ds(0, 31)], st_s.at[2])
    take(sin2.at[pl.ds(0, 15)], st_s.at[3])
    for p in range(PARTS):
        take(core_out[p], core_s.at[p])
        take(cut[p].at[pl.ds(0, RED - 1)], cut_s.at[p])
        take(mid_in[p].at[pl.ds(0, 7)], mid_s.at[p])
        take(whole[p].at[pl.ds(0, RED - 1)], who_s.at[p])
    to_sums.wait()
    to_fg.wait()
    for p in range(PARTS):
        take(whole[p], oth_s.at[p])
        keep_own(p).wait()
        take(kg_hbm[p].at[1 - c], oth_r.at[p])


def last_kernel(*refs):
    kg = refs[:PARTS]
    fg, sums, kgrad, fg_out, gain_grad, shift_grad, wide, flat, sem = refs[PARTS:]
    outs = [pltpu.make_async_copy(fg, fg_out, sem.at[9])]
    outs[0].start()
    for i, out in ((0, shift_grad), (1, gain_grad)):
        for half in range(2):
            flat[i, pl.ds(half * 128, 128)] = sums[2 * i + half]
        outs.append(pltpu.make_async_copy(flat.at[i], out, sem.at[10 + i]))
        outs[-1].start()
    for p in range(PARTS):
        for k, tap in enumerate(TAPS[p]):
            at = pl.ds(tap * CH, CH)
            for half in range(2):
                v = kg[p][half].astype(F32).reshape(RED * PIECES[p], 128)
                wide[at, pl.ds(half * 128, 128)] = v[k * CH : (k + 1) * CH]
            outs.append(pltpu.make_async_copy(wide.at[at], kgrad.at[at], sem.at[tap]))
            outs[-1].start()
    for out in outs:
        out.wait()


def local(features, cotangent, kernel, norm_gain, norm_shift):
    any_spec = pl.BlockSpec(memory_space=pl.ANY)
    vmem = pltpu.VMEM
    dma = pltpu.SemaphoreType.DMA
    features, cotangent, kernel, norm_gain, norm_shift = [
        pltpu.with_memory_space_constraint(v, pltpu.HBM)
        for v in (features, cotangent, kernel.reshape(9, CH, CH), norm_gain, norm_shift)
    ]
    rows = [RED * piece for piece in PIECES]
    shared = [(RED, piece, 128) for piece in PIECES]
    fg, sums, *kg = pl.pallas_call(
        main_kernel,
        out_shape=[
            jax.ShapeDtypeStruct((ROWS, COLS, CH), BF16),
            jax.ShapeDtypeStruct((4, 128), F32),
        ]
        + [jax.ShapeDtypeStruct((2,) + shape, BF16) for shape in shared],
        in_specs=[pl.BlockSpec(memory_space=pltpu.HBM)] * 5,
        out_specs=[any_spec] * (2 + PARTS),
        scratch_shapes=[
            vmem((ROWS, COLS, CH), BF16),
            vmem((ROWS, COLS, CH), BF16),
            vmem((9, CH, CH), BF16),
            vmem((CH,), F32),
            vmem((CH,), F32),
            vmem((ROWS, COLS, CH), BF16),
            vmem((3, 2, CELLS + 16, 128), F32),
            vmem((3, CELLS, CH), BF16),
            vmem((3, CELLS + 16, CH), BF16),
            vmem((3, 128, CH), BF16),
            vmem((CELLS, CH), F32),
            vmem((CH, CELLS), BF16),
            vmem((2, ROWS, CH), BF16),
            vmem((2, ROWS, CH), BF16),
            vmem((2, 3, 8, CH), F32),
            vmem((2, 3, 8, CH), F32),
            vmem((2, 3, 8, CH), F32),
            vmem((4, 128), F32),
            vmem((32, 4, 128), F32),
            vmem((4, 128), F32),
            vmem((16, 4, 128), F32),
            vmem((4, 128), F32),
            vmem((32, 4, 128), F32),
            vmem((4, 128), F32),
            vmem((16, 4, 128), F32),
            vmem((4, 128), F32),
            *[vmem((n, 128), F32) for n in rows],
            *[vmem((n, 128), BF16) for n in rows],
            *[vmem((n, 128), BF16) for n in rows],
            *[vmem(shape, BF16) for shape in shared],
            *[vmem(shape, BF16) for shape in shared],
            *[vmem((piece, 128), BF16) for piece in PIECES],
            *[vmem((8, piece, 128), BF16) for piece in PIECES],
            *[vmem(shape, BF16) for shape in shared],
            pltpu.SemaphoreType.REGULAR,
            dma((5,)),
            dma((PARTS + 2,)),
            dma((2,)), dma((2,)),
            dma((3,)), dma((3,)),
            dma((4,)), dma((4,)),
            dma((PARTS,)), dma((PARTS,)),
            dma((PARTS,)), dma((PARTS,)),
            dma((PARTS,)), dma((PARTS,)),
            dma((PARTS,)), dma((PARTS,)),
            dma((PARTS,)), dma((PARTS,)),
        ],
        compiler_params=pltpu.CompilerParams(
            collective_id=0, has_side_effects=True, vmem_limit_bytes=48 * 2**20
        ),
        name="backward",
    )(features, cotangent, kernel, norm_gain, norm_shift)
    in_vmem = pl.BlockSpec(memory_space=pltpu.VMEM)
    kgrad, fg, gain_grad, shift_grad = pl.pallas_call(
        last_kernel,
        out_shape=(
            jax.ShapeDtypeStruct((9 * CH, CH), F32),
            jax.ShapeDtypeStruct((ROWS, COLS, CH), BF16),
            jax.ShapeDtypeStruct((CH,), F32),
            jax.ShapeDtypeStruct((CH,), F32),
        ),
        in_specs=[in_vmem] * (PARTS + 2),
        out_specs=(any_spec,) * 4,
        scratch_shapes=[vmem((9 * CH, CH), F32), vmem((2, CH), F32), dma((12,))],
        compiler_params=pltpu.CompilerParams(vmem_limit_bytes=16 * 2**20),
        name="outputs",
    )(*kg, fg, sums)
    return fg, kgrad.reshape(3, 3, CH, CH), gain_grad, shift_grad


def solution(mesh):
    placed = (P("lat", "lon", None), P("lat", "lon", None), P(), P(), P())
    return jax.shard_map(
        local,
        mesh=mesh,
        in_specs=placed,
        out_specs=(P("lat", "lon", None), P(), P(), P()),
        check_vma=False,
    )
```
